32 devices in a mesh: gx: 4 (over y, core), gy: 8 (over z, x).
Axes of the slice: x: 2, y: 2, z: 4, core: 2. Of those that a mesh axis runs over, the one named last changes fastest.
Arguments:
- rhs_blocks: bfloat16 [32, 64, 64, 128], P('gx', 'gy'), may hold values from -6 to 6
- diag_factor: bfloat16 [32, 64, 128, 128], P('gx', 'gy'), as said below
- cond_factor: bfloat16 [32, 64, 6, 128, 128], P('gx', 'gy'), may hold values from -0.21875 to 0.21875
- cond: int32 [32, 64, 6], P('gx', 'gy'), may hold values from 0 to 24, as said below
Outputs:
- precision_times: float32 [32, 64, 64, 128], P('gx', 'gy')
The draws below stay inside these ranges and needn't reach their ends.
Inputs may be any that keep to these rules, and one draw needn't show every extreme that they name: `cond`: each block's 6 codes are distinct, never 12, and name blocks inside the grid of 32 x 64 blocks. `diag_factor`: each matrix is upper triangular with a positive diagonal.
All inputs are finite; a program needn't handle non-finite values.
Results may differ from the reference program's by a relative error of at most 0.0023.
Values may be sent and summed in bfloat16 or wider, within the bound.
A program may use at most 192 MiB of HBM per device.

```python
import jax
import jax.numpy as jnp
from jax import lax

POINTS = 128
RHS = 64
CONDS = 6
BLOCKS_X = 32
BLOCKS_Y = 64


def draw_diag_factor(key, part):
    base = jax.random.fold_in(key, 11)
    key_off, key_diag = jax.random.split(base)
    shape = (BLOCKS_X, BLOCKS_Y, POINTS, POINTS)
    off_values = 0.09 * jax.random.normal(key_off, shape, jnp.float32)
    diag_values = jax.random.uniform(key_diag, shape, jnp.float32, 0.5, 2.0)
    row_ids = lax.broadcasted_iota(jnp.int32, shape, 2)
    col_ids = lax.broadcasted_iota(jnp.int32, shape, 3)
    upper = jnp.where(col_ids > row_ids, off_values, 0.0)
    return jnp.where(col_ids == row_ids, diag_values, upper).astype(jnp.bfloat16)


def draw_cond(key, part):
    base = jax.random.fold_in(key, 23)
    shape = (BLOCKS_X, BLOCKS_Y, 25)
    codes = lax.broadcasted_iota(jnp.int32, shape, 2)
    row_ids = lax.broadcasted_iota(jnp.int32, shape, 0) + codes // 5 - 2
    col_ids = lax.broadcasted_iota(jnp.int32, shape, 1) + codes % 5 - 2
    valid = (row_ids >= 0) & (row_ids < BLOCKS_X) & (col_ids >= 0) & (col_ids < BLOCKS_Y) & (codes != 12)
    scores = jax.random.randint(base, shape, 0, 1 << 20) * 32 + codes
    scores = jnp.where(valid, scores, -1 - codes)
    chosen = lax.top_k(scores, CONDS)[1]
    return chosen.astype(jnp.int32)


def block_levels(stream_key, extent, pieces, least, high):
    loudness = 1.0
    for position, parts in pieces:
        steps = jax.random.uniform(jax.random.fold_in(jax.random.fold_in(stream_key, 6), position), (parts,), jnp.float32, least / len(pieces), high / len(pieces))
        loudness = loudness * jnp.repeat(jnp.exp(steps), extent[position] // parts).reshape((-1,) + (1,) * (len(extent) - 1 - position))
    return loudness


def noise(key, shape, scale, bound, pieces=(), held_as=jnp.bfloat16):
    gain = block_levels(key, shape, pieces, -0.22, 0.18) if pieces else 1.0
    entries = jax.random.normal(key, shape, jnp.float32) * scale * gain
    return jnp.minimum(jnp.maximum(entries, -bound), bound).astype(held_as)


def setup_inputs(seed: int = 0) -> dict:
    key_of = jax.random.split(jax.random.key(seed), 5)
    rhs_blocks = noise(key_of[0], (BLOCKS_X, BLOCKS_Y, RHS, POINTS), 1.0, 6.0, ((0, 4), (1, 8)))
    diag_factor = draw_diag_factor(jax.random.fold_in(key_of[4], 71), 0)
    cond_factor = noise(key_of[2], (BLOCKS_X, BLOCKS_Y, CONDS, POINTS, POINTS), (CONDS * POINTS) ** -0.5, 0.21875, ((0, 4), (1, 8)))
    cond = draw_cond(jax.random.fold_in(key_of[4], 71), 0)
    return {"rhs_blocks": rhs_blocks, "diag_factor": diag_factor, "cond_factor": cond_factor, "cond": cond}


def reference(rhs_blocks, diag_factor, cond_factor, cond):
    padded = jnp.pad(rhs_blocks, ((2, 2), (2, 2), (0, 0), (0, 0)))
    padded_cols = BLOCKS_Y + 4
    col_ids = jnp.arange(BLOCKS_Y, dtype=jnp.int32)[:, None]
    row_list = jnp.arange(BLOCKS_X, dtype=jnp.int32)

    def slots_of(row_index):
        codes = cond[row_index]
        return (codes // 5) * padded_cols + col_ids + codes % 5

    def forward_row(row_index):
        window = lax.dynamic_slice_in_dim(padded, row_index, 5, 0).reshape((5 * padded_cols, RHS, POINTS))
        picked = window[slots_of(row_index)]
        own_part = jnp.einsum("yrp,ypq->yrq", rhs_blocks[row_index].astype(jnp.float32), diag_factor[row_index].astype(jnp.float32))
        far_part = jnp.einsum("ykrp,ykpq->yrq", picked.astype(jnp.float32), cond_factor[row_index].astype(jnp.float32))
        return (own_part + far_part).astype(jnp.bfloat16)

    whitened = lax.map(forward_row, row_list)

    def backward_row(accum, row_index):
        white_row = whitened[row_index].astype(jnp.float32)
        spread = jnp.einsum("yrq,ykpq->ykrp", white_row, cond_factor[row_index].astype(jnp.float32))
        window = lax.dynamic_slice_in_dim(accum, row_index, 5, 0).reshape((5 * padded_cols, RHS, POINTS))
        window = window.at[slots_of(row_index).reshape(-1)].add(spread.reshape((-1, RHS, POINTS)))
        accum = lax.dynamic_update_slice_in_dim(accum, window.reshape((5, padded_cols, RHS, POINTS)), row_index, 0)
        own_part = jnp.einsum("yrq,ypq->yrp", white_row, diag_factor[row_index].astype(jnp.float32))
        return accum, own_part

    start = jnp.zeros((BLOCKS_X + 4, padded_cols, RHS, POINTS), jnp.float32)
    accum, owns = lax.scan(backward_row, start, row_list)
    return owns + accum[2:BLOCKS_X + 2, 2:BLOCKS_Y + 2]
```

```python
import functools

import jax
import jax.numpy as jnp
from jax import lax
from jax.experimental import pallas as pl
from jax.experimental.pallas import tpu as pltpu
from jax.sharding import PartitionSpec as P

MESH = pl.DeviceIdType.MESH
REACH = 2
SPAN = 2 * REACH + 1
SIDES = [(0, -1), (0, 1), (-1, 0), (1, 0), (-1, -1), (-1, 1), (1, -1), (1, 1)]


def own_edge(step, size):
    return {-1: (0, REACH), 0: (0, size), 1: (size - REACH, REACH)}[step]


def outer_edge(step, size):
    return {-1: (0, REACH), 0: (REACH, size), 1: (REACH + size, REACH)}[step]


def at_region(ref, row_part, col_part):
    return ref.at[pl.ds(*row_part), pl.ds(*col_part)]


def neighbourhood():
    row, col = lax.axis_index("gx"), lax.axis_index("gy")
    rows, cols = lax.axis_size("gx"), lax.axis_size("gy")

    def inside(side):
        r, c = row + side[0], col + side[1]
        return (r >= 0) & (r < rows) & (c >= 0) & (c < cols)

    def device(side):
        return {"gx": row + side[0], "gy": col + side[1]}

    return inside, device


def greet(inside, device):
    barrier = pltpu.get_barrier_semaphore()
    count = jnp.int32(0)
    for side in SIDES:
        count = count + inside(side).astype(jnp.int32)

        @pl.when(inside(side))
        def _():
            pl.semaphore_signal(barrier, inc=1, device_id=device(side), device_id_type=MESH)

    pl.semaphore_wait(barrier, count)


def opposite(side):
    return (-side[0], -side[1])


def forward_kernel(rhs, diag, far, cond, white, local, padded, weights, load_sem, rhs_sem, send_sem, recv_sem):
    tile_rows, tile_cols, count_rhs, points = rhs.shape
    depth = far.shape[2]
    inside, device = neighbourhood()
    row_order = list(range(REACH, tile_rows - REACH))
    row_order += [r for r in range(tile_rows) if r not in row_order]

    def loads(r):
        return [
            pltpu.make_async_copy(far.at[r], weights.at[r, :, pl.ds(0, depth)], load_sem.at[r, 0]),
            pltpu.make_async_copy(diag.at[r], weights.at[r, :, pl.ds(depth, points)], load_sem.at[r, 1]),
        ]

    local_copy = pltpu.make_async_copy(rhs, local, rhs_sem.at[0])
    centre_copy = pltpu.make_async_copy(
        rhs, at_region(padded, (REACH, tile_rows), (REACH, tile_cols)), rhs_sem.at[1]
    )
    local_copy.start()
    for r in row_order[:1]:
        for copy in loads(r):
            copy.start()

    def remote(index):
        side = SIDES[index]
        back = opposite(side)
        return pltpu.make_async_remote_copy(
            src_ref=at_region(rhs, own_edge(side[0], tile_rows), own_edge(side[1], tile_cols)),
            dst_ref=at_region(padded, outer_edge(back[0], tile_rows), outer_edge(back[1], tile_cols)),
            send_sem=send_sem.at[index],
            recv_sem=recv_sem.at[index],
            device_id=device(side),
            device_id_type=MESH,
        )

    greet(inside, device)
    for index, side in enumerate(SIDES):

        @pl.when(inside(side))
        def _():
            remote(index).start()

    centre_copy.start()
    for r in row_order[1:]:
        for copy in loads(r):
            copy.start()

    def mix(source, shift, r, c):
        parts = []
        for k in range(depth // points):
            code = cond[r, c, k]
            parts.append(source[r + code // SPAN + shift, c + lax.rem(code, SPAN) + shift])
        parts.append(source[r + REACH + shift, c + REACH + shift])
        mixed = jnp.dot(
            jnp.concatenate(parts, axis=1), weights[r, c], preferred_element_type=jnp.float32
        )
        white[r, c] = mixed.astype(white.dtype)

    inner_cols = list(range(REACH, tile_cols - REACH))
    outer_cols = [c for c in range(tile_cols) if c not in inner_cols]

    local_copy.wait()
    for r in range(REACH, tile_rows - REACH):
        for copy in loads(r):
            copy.wait()

    @pl.loop(REACH, tile_rows - REACH)
    def _(r):
        for c in inner_cols:
            mix(local, -REACH, r, c)

    centre_copy.wait()
    for r in range(tile_rows):
        if r < REACH or r >= tile_rows - REACH:
            for copy in loads(r):
                copy.wait()
    for index, side in enumerate(SIDES):

        @pl.when(inside(opposite(side)))
        def _():
            remote(index).wait_recv()

    @pl.loop(REACH, tile_rows - REACH)
    def _(r):
        for c in outer_cols:
            mix(padded, 0, r, c)

    @pl.loop(0, 2 * REACH)
    def _(step):
        r = jnp.where(step < REACH, step, tile_rows - 2 * REACH + step)
        for c in range(tile_cols):
            mix(padded, 0, r, c)

    for index, side in enumerate(SIDES):

        @pl.when(inside(side))
        def _():
            remote(index).wait_send()


def backward_kernel(white, diag, far, cond, own, halo, total):
    r = pl.program_id(0)
    tile_rows = pl.num_programs(0)
    tile_cols, count_rhs, points = white.shape[1:]
    conds = far.shape[2] // points
    across = (((1,), (1,)), ((), ()))

    @pl.when(r == 0)
    def _():
        @pl.loop(0, total.shape[0])
        def _(i):
            total[i] = jnp.zeros(total.shape[1:], jnp.float32)

    for c in range(tile_cols):
        value = white[0, c]
        spread = lax.dot_general(value, far[0, c], across, preferred_element_type=jnp.float32)
        kept = lax.dot_general(value, diag[0, c], across, preferred_element_type=jnp.float32)
        places = []
        for k in range(conds):
            code = cond[r, c, k]
            places.append((r + code // SPAN, c + lax.rem(code, SPAN)))
        places.append((r + REACH, c + REACH))
        held = [total[i, j] for i, j in places]
        for k, (i, j) in enumerate(places):
            term = kept if k == conds else spread[:, k * points : (k + 1) * points]
            total[i, j] = held[k] + term

    @pl.when(r == tile_rows - 1)
    def _():
        rows = own.shape[0]

        @pl.loop(0, rows + 2 * REACH)
        def _(i):
            for j in list(range(REACH)) + list(range(tile_cols + REACH, tile_cols + 2 * REACH)):
                halo[i, j] = total[i, j].astype(halo.dtype)

        @pl.loop(0, 2 * REACH)
        def _(step):
            i = jnp.where(step < REACH, step, rows + step)
            for j in range(REACH, tile_cols + REACH):
                halo[i, j] = total[i, j].astype(halo.dtype)

        @pl.loop(0, rows)
        def _(i):
            for j in range(tile_cols):
                own[i, j] = total[i + REACH, j + REACH]


def exchange_kernel(halo, *refs):
    landings, (send_sem, recv_sem) = refs[: len(SIDES)], refs[len(SIDES) :]
    tile_rows, tile_cols = halo.shape[0] - 2 * REACH, halo.shape[1] - 2 * REACH
    inside, device = neighbourhood()

    def remote(index):
        side = SIDES[index]
        return pltpu.make_async_remote_copy(
            src_ref=at_region(halo, outer_edge(side[0], tile_rows), outer_edge(side[1], tile_cols)),
            dst_ref=landings[index],
            send_sem=send_sem.at[index],
            recv_sem=recv_sem.at[index],
            device_id=device(side),
            device_id_type=MESH,
        )

    greet(inside, device)
    for index, side in enumerate(SIDES):

        @pl.when(inside(side))
        def _():
            remote(index).start()

    for index, side in enumerate(SIDES):

        @pl.when(inside(opposite(side)))
        def _():
            remote(index).wait_recv()

        @pl.when(inside(side))
        def _():
            remote(index).wait_send()


def finish_kernel(own, *refs):
    landings, out = refs[: len(SIDES)], refs[len(SIDES)]
    tile_rows, tile_cols = own.shape[:2]
    inside, _ = neighbourhood()

    @pl.loop(0, tile_rows)
    def _(i):
        out[i] = own[i]

    for index, side in enumerate(SIDES):
        back = opposite(side)
        row_start, row_count = own_edge(back[0], tile_rows)
        col_start, col_count = own_edge(back[1], tile_cols)

        @pl.when(inside(back))
        def _():
            @pl.loop(0, row_count)
            def _(i):
                for j in range(col_count):
                    out[row_start + i, col_start + j] += landings[index][i, j].astype(jnp.float32)


def shards(rhs_blocks, diag_factor, cond_factor, cond):
    tile_rows, tile_cols, count_rhs, points = rhs_blocks.shape
    conds = cond.shape[2]
    depth = conds * points
    far = cond_factor.reshape(tile_rows, tile_cols, depth, points)
    block = (count_rhs, points)
    padded = (tile_rows + 2 * REACH, tile_cols + 2 * REACH) + block
    anywhere = pl.BlockSpec(memory_space=pl.ANY)
    scalars = pl.BlockSpec(memory_space=pltpu.SMEM)
    whole = pl.BlockSpec(memory_space=pltpu.VMEM)
    sides = len(SIDES)
    white = pl.pallas_call(
        forward_kernel,
        out_shape=jax.ShapeDtypeStruct(rhs_blocks.shape, jnp.bfloat16),
        in_specs=[anywhere, anywhere, anywhere, scalars],
        out_specs=whole,
        scratch_shapes=[
            pltpu.VMEM(rhs_blocks.shape, rhs_blocks.dtype),
            pltpu.VMEM(padded, rhs_blocks.dtype),
            pltpu.VMEM((tile_rows, tile_cols, depth + points, points), far.dtype),
            pltpu.SemaphoreType.DMA((tile_rows, 2)),
            pltpu.SemaphoreType.DMA((2,)),
            pltpu.SemaphoreType.DMA((sides,)),
            pltpu.SemaphoreType.DMA((sides,)),
        ],
        compiler_params=pltpu.CompilerParams(
            collective_id=0, has_side_effects=True, vmem_limit_bytes=40 * 2**20
        ),
        name="forward",
    )(rhs_blocks, diag_factor, far, cond)

    own, halo = pl.pallas_call(
        backward_kernel,
        out_shape=(
            jax.ShapeDtypeStruct(rhs_blocks.shape, jnp.float32),
            jax.ShapeDtypeStruct(padded, jnp.bfloat16),
        ),
        grid=(tile_rows,),
        in_specs=[
            pl.BlockSpec((1, tile_cols) + block, lambda r: (r, 0, 0, 0)),
            pl.BlockSpec((1, tile_cols, points, points), lambda r: (r, 0, 0, 0)),
            pl.BlockSpec((1, tile_cols, depth, points), lambda r: (r, 0, 0, 0)),
            scalars,
        ],
        out_specs=(whole, whole),
        scratch_shapes=[pltpu.VMEM(padded, jnp.float32)],
        compiler_params=pltpu.CompilerParams(vmem_limit_bytes=40 * 2**20),
        name="backward",
    )(white, diag_factor, far, cond)

    landing = []
    for side in SIDES:
        part = (own_edge(side[0], tile_rows)[1], own_edge(side[1], tile_cols)[1])
        landing.append(jax.ShapeDtypeStruct(part + block, jnp.bfloat16))
    landed = pl.pallas_call(
        exchange_kernel,
        out_shape=tuple(landing),
        in_specs=[anywhere],
        out_specs=tuple(anywhere for _ in SIDES),
        scratch_shapes=[pltpu.SemaphoreType.DMA((sides,)), pltpu.SemaphoreType.DMA((sides,))],
        compiler_params=pltpu.CompilerParams(collective_id=1, has_side_effects=True),
        name="exchange",
    )(halo)

    return pl.pallas_call(
        finish_kernel,
        out_shape=jax.ShapeDtypeStruct(rhs_blocks.shape, jnp.float32),
        in_specs=[whole] * (1 + sides),
        out_specs=whole,
        compiler_params=pltpu.CompilerParams(vmem_limit_bytes=40 * 2**20),
        name="finish",
    )(own, *landed)


def solution(mesh):
    in_specs = (
        P("gx", "gy", None, None),
        P("gx", "gy", None, None),
        P("gx", "gy", None, None, None),
        P("gx", "gy", None),
    )
    out_specs = P("gx", "gy", None, None)
    return jax.shard_map(shards, mesh=mesh, in_specs=in_specs, out_specs=out_specs, check_vma=False)
```

```python
import functools

import jax
import jax.numpy as jnp
from jax import lax
from jax.experimental import pallas as pl
from jax.experimental.pallas import tpu as pltpu
from jax.sharding import PartitionSpec as P

MESH = pl.DeviceIdType.MESH
REACH = 2
SPAN = 2 * REACH + 1
ROW_SIDES = [(-1, 0), (1, 0)]
COL_SIDES = [(0, -1), (0, 1)]
SIDES = ROW_SIDES + COL_SIDES


def own_edge(step, size):
    return {-1: (0, REACH), 0: (0, size), 1: (size - REACH, REACH)}[step]


def outer_edge(step, size):
    return {-1: (0, REACH), 0: (REACH, size), 1: (REACH + size, REACH)}[step]


def at_region(ref, row_part, col_part):
    return ref.at[pl.ds(*row_part), pl.ds(*col_part)]


def neighbourhood():
    row, col = lax.axis_index("gx"), lax.axis_index("gy")
    rows, cols = lax.axis_size("gx"), lax.axis_size("gy")

    def inside(side):
        r, c = row + side[0], col + side[1]
        return (r >= 0) & (r < rows) & (c >= 0) & (c < cols)

    def device(side):
        return {"gx": row + side[0], "gy": col + side[1]}

    return inside, device


def greet(inside, device):
    barrier = pltpu.get_barrier_semaphore()
    count = jnp.int32(0)
    for side in SIDES:
        count = count + inside(side).astype(jnp.int32)

        @pl.when(inside(side))
        def _():
            pl.semaphore_signal(barrier, inc=1, device_id=device(side), device_id_type=MESH)

    pl.semaphore_wait(barrier, count)


def opposite(side):
    return (-side[0], -side[1])


def transfer(src, dst, send_sem, recv_sem, index, device, side):
    return pltpu.make_async_remote_copy(
        src_ref=src,
        dst_ref=dst,
        send_sem=send_sem.at[index],
        recv_sem=recv_sem.at[index],
        device_id=device(side),
        device_id_type=MESH,
    )


def start_if(inside, side, copies):
    @pl.when(inside(side))
    def _():
        for copy in copies():
            copy.start()


def wait_recv_if(inside, side, copies):
    @pl.when(inside(opposite(side)))
    def _():
        for copy in copies():
            copy.wait_recv()


def wait_send_if(inside, side, copies):
    @pl.when(inside(side))
    def _():
        for copy in copies():
            copy.wait_send()


def forward_kernel(rhs, diag, far, cond, white, local, rowed, padded, weights, load_sem, rhs_sem, send_sem, recv_sem):
    tile_rows, tile_cols, count_rhs, points = rhs.shape
    depth = far.shape[2]
    inside, device = neighbourhood()
    row_order = list(range(REACH, tile_rows - REACH))
    row_order += [r for r in range(tile_rows) if r not in row_order]
    sends = (send_sem, recv_sem)
    middle = (REACH, tile_rows - 2 * REACH)

    def loads(r):
        return [
            pltpu.make_async_copy(far.at[r], weights.at[r, :, pl.ds(0, depth)], load_sem.at[r, 0]),
            pltpu.make_async_copy(diag.at[r], weights.at[r, :, pl.ds(depth, points)], load_sem.at[r, 1]),
        ]

    local_copy = pltpu.make_async_copy(rhs, local, rhs_sem.at[0])
    centre_copy = pltpu.make_async_copy(rhs, rowed.at[pl.ds(REACH, tile_rows)], rhs_sem.at[1])
    padded_copy = pltpu.make_async_copy(
        rowed, padded.at[:, pl.ds(REACH, tile_cols)], rhs_sem.at[2]
    )

    def row_copies(side):
        return [
            transfer(
                rhs.at[pl.ds(*own_edge(side[0], tile_rows))],
                rowed.at[pl.ds(*outer_edge(-side[0], tile_rows))],
                *sends, 0 if side[0] < 0 else 1, device, side,
            )
        ]

    def col_copy(side, part, index):
        return transfer(
            at_region(rhs, part, own_edge(side[1], tile_cols)),
            at_region(padded, (part[0] + REACH, part[1]), outer_edge(-side[1], tile_cols)),
            *sends, index + (0 if side[1] < 0 else 1), device, side,
        )

    def col_ends(side):
        return [
            col_copy(side, own_edge(-1, tile_rows), 2),
            col_copy(side, own_edge(1, tile_rows), 4),
        ]

    def col_middle(side):
        return [col_copy(side, middle, 6)]

    def corner_copy(side, col_side):
        start, count = own_edge(side[0], tile_rows)
        cols = outer_edge(col_side[1], tile_cols)
        return transfer(
            at_region(padded, (start + REACH, count), cols),
            at_region(padded, outer_edge(-side[0], tile_rows), cols),
            *sends,
            8 + (0 if side[0] < 0 else 1) + (0 if col_side[1] < 0 else 2),
            device, side,
        )

    local_copy.start()
    for copy in loads(row_order[0]):
        copy.start()
    greet(inside, device)
    for side in COL_SIDES:
        start_if(inside, side, lambda: col_ends(side))
    for side in COL_SIDES:
        start_if(inside, side, lambda: col_middle(side))
    for side in ROW_SIDES:
        start_if(inside, side, lambda: row_copies(side))
    centre_copy.start()
    for r in row_order[1:]:
        for copy in loads(r):
            copy.start()

    def mix(source, row_shift, col_shift, r, c):
        parts = []
        for k in range(depth // points):
            code = cond[r, c, k]
            parts.append(source[r + code // SPAN + row_shift, c + lax.rem(code, SPAN) + col_shift])
        parts.append(source[r + REACH + row_shift, c + REACH + col_shift])
        mixed = jnp.dot(
            jnp.concatenate(parts, axis=1), weights[r, c], preferred_element_type=jnp.float32
        )
        white[r, c] = mixed.astype(white.dtype)

    inner_cols = list(range(REACH, tile_cols - REACH))
    outer_cols = [c for c in range(tile_cols) if c not in inner_cols]

    local_copy.wait()
    for r in range(REACH, tile_rows - REACH):
        for copy in loads(r):
            copy.wait()

    @pl.loop(REACH, tile_rows - REACH)
    def _(r):
        for c in inner_cols:
            mix(local, -REACH, -REACH, r, c)

    centre_copy.wait()
    for side in ROW_SIDES:
        wait_recv_if(inside, side, lambda: row_copies(side))
    padded_copy.start()

    for col_side in COL_SIDES:
        wait_recv_if(inside, opposite(col_side), lambda: col_ends(opposite(col_side)))
        for side in ROW_SIDES:

            @pl.when(inside(side) & inside(col_side))
            def _():
                corner_copy(side, col_side).start()

    for r in range(tile_rows):
        if r < REACH or r >= tile_rows - REACH:
            for copy in loads(r):
                copy.wait()

    @pl.loop(0, 2 * REACH)
    def _(step):
        r = jnp.where(step < REACH, step, tile_rows - 2 * REACH + step)
        for c in inner_cols:
            mix(rowed, 0, -REACH, r, c)

    padded_copy.wait()
    for side in COL_SIDES:
        wait_recv_if(inside, side, lambda: col_middle(side))
    for col_side in COL_SIDES:
        for side in ROW_SIDES:

            @pl.when(inside(opposite(side)) & inside(col_side))
            def _():
                corner_copy(side, col_side).wait_recv()

    @pl.loop(0, tile_rows)
    def _(r):
        for c in outer_cols:
            mix(padded, 0, 0, r, c)

    for side in COL_SIDES:
        wait_send_if(inside, side, lambda: col_ends(side) + col_middle(side))
    for side in ROW_SIDES:
        wait_send_if(inside, side, lambda: row_copies(side))
        for col_side in COL_SIDES:

            @pl.when(inside(side) & inside(col_side))
            def _():
                corner_copy(side, col_side).wait_send()


def backward_kernel(white, diag, far, cond, own, halo, total):
    r = pl.program_id(0)
    tile_cols, count_rhs, points = white.shape[1:]
    tile_rows = pl.num_programs(0) - 2 * REACH
    conds = far.shape[2] // points
    across = (((1,), (1,)), ((), ()))

    def clear(i):
        total[i] = jnp.zeros(total.shape[1:], jnp.float32)

    @pl.when(r == 0)
    def _():
        pl.loop(0, 2 * REACH)(clear)

    @pl.when(r < tile_rows)
    def _():
        clear(r + 2 * REACH)
        for c in range(tile_cols):
            value = white[0, c]
            spread = lax.dot_general(value, far[0, c], across, preferred_element_type=jnp.float32)
            kept = lax.dot_general(value, diag[0, c], across, preferred_element_type=jnp.float32)
            places = []
            for k in range(conds):
                code = cond[r, c, k]
                places.append((r + code // SPAN, c + lax.rem(code, SPAN)))
            places.append((r + REACH, c + REACH))
            held = [total[i, j] for i, j in places]
            for k, (i, j) in enumerate(places):
                term = kept if k == conds else spread[:, k * points : (k + 1) * points]
                total[i, j] = held[k] + term

    for j in range(tile_cols + 2 * REACH):
        halo[0, j] = total[r, j].astype(halo.dtype)
    @pl.when(r < tile_rows + REACH)
    def _():
        for j in range(tile_cols):
            own[0, j] = total[r, j + REACH]


def exchange_kernel(halo, landed_up, landed_down, landed_left, landed_right, edges, corners, edge_sem, send_sem, recv_sem):
    tile_rows, tile_cols = landed_left.shape[0], landed_up.shape[1]
    inside, device = neighbourhood()
    sends = (send_sem, recv_sem)
    middle = (REACH, tile_rows - 2 * REACH)

    def place(side):
        return 0 if side[0] + side[1] < 0 else 1

    def row_copies(side):
        return [
            transfer(
                at_region(halo, outer_edge(side[0], tile_rows), (REACH, tile_cols)),
                landed_down if side[0] < 0 else landed_up,
                *sends, place(side), device, side,
            )
        ]

    def corner_copies(side):
        return [
            transfer(
                at_region(halo, outer_edge(side[0], tile_rows), outer_edge(col_side[1], tile_cols)),
                corners.at[place(opposite(side)), place(col_side)],
                *sends, 2 + place(side) + 2 * place(col_side), device, side,
            )
            for col_side in COL_SIDES
        ]

    def col_landing(side):
        return landed_right if side[1] < 0 else landed_left

    def col_middle(side):
        return [
            transfer(
                at_region(halo, (middle[0] + REACH, middle[1]), outer_edge(side[1], tile_cols)),
                col_landing(side).at[pl.ds(*middle)],
                *sends, 6 + place(side), device, side,
            )
        ]

    def col_end(side, row_side):
        return transfer(
            edges.at[place(row_side), place(side)],
            col_landing(side).at[pl.ds(*own_edge(row_side[0], tile_rows))],
            *sends, 8 + place(side) + 2 * place(row_side), device, side,
        )

    def col_ends(side):
        return [col_end(side, row_side) for row_side in ROW_SIDES]

    def edge_copy(row_side, side):
        start, count = own_edge(row_side[0], tile_rows)
        return pltpu.make_async_copy(
            at_region(halo, (start + REACH, count), outer_edge(side[1], tile_cols)),
            edges.at[place(row_side), place(side)],
            edge_sem.at[place(row_side) + 2 * place(side)],
        )

    for row_side in ROW_SIDES:
        for side in COL_SIDES:
            edge_copy(row_side, side).start()
    greet(inside, device)
    for side in ROW_SIDES:
        start_if(inside, side, lambda: corner_copies(side))
    for side in COL_SIDES:
        start_if(inside, side, lambda: col_middle(side))
    for side in ROW_SIDES:
        start_if(inside, side, lambda: row_copies(side))
    for row_side in ROW_SIDES:
        row = place(row_side)
        wait_recv_if(inside, opposite(row_side), lambda: corner_copies(opposite(row_side)))
        for side in COL_SIDES:
            col = place(side)
            edge_copy(row_side, side).wait()

            @pl.when(inside(row_side))
            def _():
                for i in range(REACH):
                    for j in range(REACH):
                        term = corners[row, col, i, j].astype(jnp.float32)
                        value = edges[row, col, i, j].astype(jnp.float32) + term
                        edges[row, col, i, j] = value.astype(edges.dtype)

            @pl.when(inside(side))
            def _():
                col_end(side, row_side).start()

    for side in ROW_SIDES:
        wait_recv_if(inside, side, lambda: row_copies(side))
        wait_send_if(inside, side, lambda: row_copies(side) + corner_copies(side))
    for side in COL_SIDES:
        wait_recv_if(inside, side, lambda: col_middle(side) + col_ends(side))
        wait_send_if(inside, side, lambda: col_middle(side) + col_ends(side))


def finish_kernel(own, landed_up, landed_down, landed_left, landed_right, out):
    r = pl.program_id(0)
    tile_rows, tile_cols = pl.num_programs(0), own.shape[1]
    inside, _ = neighbourhood()
    out[...] = own[...]

    for side, landed in zip(COL_SIDES, (landed_left, landed_right)):
        start, count = own_edge(side[1], tile_cols)

        @pl.when(inside(side))
        def _():
            out[0, pl.ds(start, count)] += landed[r].astype(jnp.float32)

    for side, landed in zip(ROW_SIDES, (landed_up, landed_down)):
        start, count = own_edge(side[0], tile_rows)

        @pl.when(inside(side) & (r >= start) & (r < start + count))
        def _():
            out[0] += landed[r - start].astype(jnp.float32)


def shards(rhs_blocks, diag_factor, cond_factor, cond):
    tile_rows, tile_cols, count_rhs, points = rhs_blocks.shape
    conds = cond.shape[2]
    depth = conds * points
    far = cond_factor.reshape(tile_rows, tile_cols, depth, points)
    block = (count_rhs, points)
    padded = (tile_rows + 2 * REACH, tile_cols + 2 * REACH) + block
    anywhere = pl.BlockSpec(memory_space=pltpu.HBM)
    scalars = pl.BlockSpec(memory_space=pltpu.SMEM)
    whole = pl.BlockSpec(memory_space=pltpu.VMEM)
    transfers = 12
    white = pl.pallas_call(
        forward_kernel,
        out_shape=jax.ShapeDtypeStruct(rhs_blocks.shape, jnp.bfloat16),
        in_specs=[anywhere, anywhere, anywhere, scalars],
        out_specs=whole,
        scratch_shapes=[
            pltpu.VMEM(rhs_blocks.shape, rhs_blocks.dtype),
            pltpu.VMEM((tile_rows + 2 * REACH, tile_cols) + block, rhs_blocks.dtype),
            pltpu.VMEM(padded, rhs_blocks.dtype),
            pltpu.VMEM((tile_rows, tile_cols, depth + points, points), far.dtype),
            pltpu.SemaphoreType.DMA((tile_rows, 2)),
            pltpu.SemaphoreType.DMA((3,)),
            pltpu.SemaphoreType.DMA((transfers,)),
            pltpu.SemaphoreType.DMA((transfers,)),
        ],
        compiler_params=pltpu.CompilerParams(
            collective_id=0, has_side_effects=True, vmem_limit_bytes=63 * 2**20
        ),
        name="forward",
    )(rhs_blocks, diag_factor, far, cond)

    own, halo = pl.pallas_call(
        backward_kernel,
        out_shape=(
            jax.ShapeDtypeStruct(rhs_blocks.shape, jnp.float32),
            jax.ShapeDtypeStruct(padded, jnp.bfloat16),
        ),
        grid=(tile_rows + 2 * REACH,),
        in_specs=[
            pl.BlockSpec((1, tile_cols) + block, lambda r: (jnp.minimum(r, tile_rows - 1), 0, 0, 0)),
            pl.BlockSpec((1, tile_cols, points, points), lambda r: (jnp.minimum(r, tile_rows - 1), 0, 0, 0)),
            pl.BlockSpec((1, tile_cols, depth, points), lambda r: (jnp.minimum(r, tile_rows - 1), 0, 0, 0)),
            scalars,
        ],
        out_specs=(
            pl.BlockSpec((1, tile_cols) + block, lambda r: (jnp.clip(r - REACH, 0, tile_rows - 1), 0, 0, 0)),
            pl.BlockSpec((1, tile_cols + 2 * REACH) + block, lambda r: (r, 0, 0, 0)),
        ),
        scratch_shapes=[pltpu.VMEM(padded, jnp.float32)],
        compiler_params=pltpu.CompilerParams(vmem_limit_bytes=63 * 2**20),
        name="backward",
    )(white, diag_factor, far, cond)

    row_part = jax.ShapeDtypeStruct((REACH, tile_cols) + block, jnp.bfloat16)
    col_part = jax.ShapeDtypeStruct((tile_rows, REACH) + block, jnp.bfloat16)
    landed = pl.pallas_call(
        exchange_kernel,
        out_shape=(row_part, row_part, col_part, col_part),
        in_specs=[anywhere],
        out_specs=(whole,) * 4,
        scratch_shapes=[
            pltpu.VMEM((2, 2, REACH, REACH) + block, jnp.bfloat16),
            pltpu.VMEM((2, 2, REACH, REACH) + block, jnp.bfloat16),
            pltpu.SemaphoreType.DMA((4,)),
            pltpu.SemaphoreType.DMA((transfers,)),
            pltpu.SemaphoreType.DMA((transfers,)),
        ],
        compiler_params=pltpu.CompilerParams(
            collective_id=1, has_side_effects=True, vmem_limit_bytes=62 * 2**20
        ),
        name="exchange",
    )(halo)

    return pl.pallas_call(
        finish_kernel,
        out_shape=jax.ShapeDtypeStruct(rhs_blocks.shape, jnp.float32),
        grid=(tile_rows,),
        in_specs=[pl.BlockSpec((1, tile_cols) + block, lambda r: (r, 0, 0, 0))] + [whole] * 4,
        out_specs=pl.BlockSpec((1, tile_cols) + block, lambda r: (r, 0, 0, 0)),
        compiler_params=pltpu.CompilerParams(vmem_limit_bytes=62 * 2**20),
        name="finish",
    )(own, *landed)


def solution(mesh):
    in_specs = (
        P("gx", "gy", None, None),
        P("gx", "gy", None, None),
        P("gx", "gy", None, None, None),
        P("gx", "gy", None),
    )
    out_specs = P("gx", "gy", None, None)
    return jax.shard_map(shards, mesh=mesh, in_specs=in_specs, out_specs=out_specs, check_vma=False)
```

```python
import functools

import jax
import jax.numpy as jnp
from jax import lax
from jax.experimental import pallas as pl
from jax.experimental.pallas import tpu as pltpu
from jax.sharding import PartitionSpec as P

MESH = pl.DeviceIdType.MESH
REACH = 2
SPAN = 2 * REACH + 1
ACROSS = (((1,), (1,)), ((), ()))
ROW_SIDES = [(-1, 0), (1, 0)]
COL_SIDES = [(0, -1), (0, 1)]
SIDES = ROW_SIDES + COL_SIDES


def own_edge(step, size):
    return {-1: (0, REACH), 0: (0, size), 1: (size - REACH, REACH)}[step]


def outer_edge(step, size):
    return {-1: (0, REACH), 0: (REACH, size), 1: (REACH + size, REACH)}[step]


def at_region(ref, row_part, col_part):
    return ref.at[pl.ds(*row_part), pl.ds(*col_part)]


def neighbourhood():
    row, col = lax.axis_index("gx"), lax.axis_index("gy")
    rows, cols = lax.axis_size("gx"), lax.axis_size("gy")

    def inside(side):
        r, c = row + side[0], col + side[1]
        return (r >= 0) & (r < rows) & (c >= 0) & (c < cols)

    def device(side):
        return {"gx": row + side[0], "gy": col + side[1]}

    return inside, device


def greet(inside, device):
    barrier = pltpu.get_barrier_semaphore()
    count = jnp.int32(0)
    for side in SIDES:
        count = count + inside(side).astype(jnp.int32)

        @pl.when(inside(side))
        def _():
            pl.semaphore_signal(barrier, inc=1, device_id=device(side), device_id_type=MESH)

    pl.semaphore_wait(barrier, count)


def opposite(side):
    return (-side[0], -side[1])


def transfer(src, dst, send_sem, recv_sem, index, device, side):
    return pltpu.make_async_remote_copy(
        src_ref=src,
        dst_ref=dst,
        send_sem=send_sem.at[index],
        recv_sem=recv_sem.at[index],
        device_id=device(side),
        device_id_type=MESH,
    )


def start_if(inside, side, copies):
    @pl.when(inside(side))
    def _():
        for copy in copies():
            copy.start()


def wait_recv_if(inside, side, copies):
    @pl.when(inside(opposite(side)))
    def _():
        for copy in copies():
            copy.wait_recv()


def wait_send_if(inside, side, copies):
    @pl.when(inside(side))
    def _():
        for copy in copies():
            copy.wait_send()


def forward_kernel(
    rhs, diag, far, cond, white, spread_out, local, rowed, padded, weights, spread, spread_sem, load_sem, rhs_sem, send_sem, recv_sem
):
    tile_rows, tile_cols, count_rhs, points = rhs.shape
    depth = far.shape[2]
    inside, device = neighbourhood()
    row_order = list(range(REACH, tile_rows - REACH))
    row_order += [r for r in range(tile_rows) if r not in row_order]
    sends = (send_sem, recv_sem)
    middle = (REACH, tile_rows - 2 * REACH)

    def loads(r):
        return [
            pltpu.make_async_copy(far.at[r], weights.at[r, :, pl.ds(0, depth)], load_sem.at[r, 0]),
            pltpu.make_async_copy(diag.at[r], weights.at[r, :, pl.ds(depth, points)], load_sem.at[r, 1]),
        ]

    local_copy = pltpu.make_async_copy(rhs, local, rhs_sem.at[0])
    centre_copy = pltpu.make_async_copy(rhs, rowed.at[pl.ds(REACH, tile_rows)], rhs_sem.at[1])
    padded_copy = pltpu.make_async_copy(
        rowed, padded.at[:, pl.ds(REACH, tile_cols)], rhs_sem.at[2]
    )

    def row_copies(side):
        return [
            transfer(
                rhs.at[pl.ds(*own_edge(side[0], tile_rows))],
                rowed.at[pl.ds(*outer_edge(-side[0], tile_rows))],
                *sends, 0 if side[0] < 0 else 1, device, side,
            )
        ]

    def col_copy(side, part, index):
        return transfer(
            at_region(rhs, part, own_edge(side[1], tile_cols)),
            at_region(padded, (part[0] + REACH, part[1]), outer_edge(-side[1], tile_cols)),
            *sends, index + (0 if side[1] < 0 else 1), device, side,
        )

    def col_ends(side):
        return [
            col_copy(side, own_edge(-1, tile_rows), 2),
            col_copy(side, own_edge(1, tile_rows), 4),
        ]

    def col_middle(side):
        return [col_copy(side, middle, 6)]

    def corner_copy(side, col_side):
        start, count = own_edge(side[0], tile_rows)
        cols = outer_edge(col_side[1], tile_cols)
        return transfer(
            at_region(padded, (start + REACH, count), cols),
            at_region(padded, outer_edge(-side[0], tile_rows), cols),
            *sends,
            8 + (0 if side[0] < 0 else 1) + (0 if col_side[1] < 0 else 2),
            device, side,
        )

    local_copy.start()
    for copy in loads(row_order[0]):
        copy.start()
    greet(inside, device)
    for side in COL_SIDES:
        start_if(inside, side, lambda: col_ends(side))
    for side in COL_SIDES:
        start_if(inside, side, lambda: col_middle(side))
    for side in ROW_SIDES:
        start_if(inside, side, lambda: row_copies(side))
    centre_copy.start()
    for r in row_order[1:]:
        for copy in loads(r):
            copy.start()

    def mix(source, row_shift, col_shift, r, c):
        parts = []
        for k in range(depth // points):
            code = cond[k, r, c]
            parts.append(source[r + code // SPAN + row_shift, c + lax.rem(code, SPAN) + col_shift])
        parts.append(source[r + REACH + row_shift, c + REACH + col_shift])
        mixed = jnp.dot(
            jnp.concatenate(parts, axis=1), weights[r, c], preferred_element_type=jnp.float32
        )
        return mixed.astype(white.dtype)

    def spread_copy(r):
        return pltpu.make_async_copy(spread.at[r], spread_out.at[r], spread_sem.at[r])

    def inner_row(source, row_shift, r):
        for index, c in enumerate(inner_cols):
            value = mix(source, row_shift, -REACH, r, c)
            spread[r, index] = lax.dot_general(
                value, weights[r, c], ACROSS, preferred_element_type=jnp.float32
            )
        spread_copy(r).start()

    inner_cols = list(range(REACH, tile_cols - REACH))
    outer_cols = [c for c in range(tile_cols) if c not in inner_cols]

    local_copy.wait()
    for r in range(REACH, tile_rows - REACH):
        for copy in loads(r):
            copy.wait()

    @pl.loop(REACH, tile_rows - REACH)
    def _(r):
        inner_row(local, -REACH, r)

    centre_copy.wait()
    for side in ROW_SIDES:
        wait_recv_if(inside, side, lambda: row_copies(side))
    padded_copy.start()

    for col_side in COL_SIDES:
        wait_recv_if(inside, opposite(col_side), lambda: col_ends(opposite(col_side)))
        for side in ROW_SIDES:

            @pl.when(inside(side) & inside(col_side))
            def _():
                corner_copy(side, col_side).start()

    for r in range(tile_rows):
        if r < REACH or r >= tile_rows - REACH:
            for copy in loads(r):
                copy.wait()

    @pl.loop(0, 2 * REACH)
    def _(step):
        r = jnp.where(step < REACH, step, tile_rows - 2 * REACH + step)
        inner_row(rowed, 0, r)

    padded_copy.wait()
    for side in COL_SIDES:
        wait_recv_if(inside, side, lambda: col_middle(side))
    for col_side in COL_SIDES:
        for side in ROW_SIDES:

            @pl.when(inside(opposite(side)) & inside(col_side))
            def _():
                corner_copy(side, col_side).wait_recv()

    @pl.loop(0, tile_rows)
    def _(r):
        for index, c in enumerate(outer_cols):
            white[r, index] = mix(padded, 0, 0, r, c)
        spread_copy(r).wait()

    for side in COL_SIDES:
        wait_send_if(inside, side, lambda: col_ends(side) + col_middle(side))
    for side in ROW_SIDES:
        wait_send_if(inside, side, lambda: row_copies(side))
        for col_side in COL_SIDES:

            @pl.when(inside(side) & inside(col_side))
            def _():
                corner_copy(side, col_side).wait_send()


def backward_kernel(
    white, diag, far, spread, cond, own, halo, weights, spreads, total, own_out, halo_out, load_sem, own_sem, halo_sem
):
    tile_rows, tile_cols, points = diag.shape[:3]
    depth = far.shape[2]
    conds = depth // points
    inner_cols = list(range(REACH, tile_cols - REACH))
    outer_cols = [c for c in range(tile_cols) if c not in inner_cols]

    def loads(r):
        copies = [pltpu.make_async_copy(spread.at[r], spreads.at[r], load_sem.at[r, 0])]
        for index, side in enumerate(COL_SIDES):
            cols = pl.ds(*own_edge(side[1], tile_cols))
            slots = pl.ds(index * REACH, REACH)
            copies += [
                pltpu.make_async_copy(
                    far.at[r, cols], weights.at[r, slots, pl.ds(0, depth)], load_sem.at[r, 1 + 2 * index]
                ),
                pltpu.make_async_copy(
                    diag.at[r, cols], weights.at[r, slots, pl.ds(depth, points)], load_sem.at[r, 2 + 2 * index]
                ),
            ]
        return copies

    @pl.loop(0, tile_rows)
    def _(r):
        for copy in loads(r):
            copy.start()

    @pl.loop(0, tile_rows + 2 * REACH)
    def _(i):
        total[i] = jnp.zeros(total.shape[1:], jnp.float32)

    def halo_copy(i):
        return pltpu.make_async_copy(halo_out.at[i], halo.at[i], halo_sem.at[i])

    def own_copy(i):
        return pltpu.make_async_copy(own_out.at[i], own.at[i], own_sem.at[i])

    def emit_halo(i):
        for j in range(tile_cols + 2 * REACH):
            halo_out[i, j] = total[i, j].astype(halo.dtype)
        halo_copy(i).start()

    def emit_own(i):
        for j in range(tile_cols):
            own_out[i, j] = total[i + REACH, j + REACH]
        own_copy(i).start()

    def add(r, c, terms):
        places = []
        for k in range(conds):
            code = cond[k, r, c]
            places.append((r + code // SPAN, c + lax.rem(code, SPAN)))
        places.append((r + REACH, c + REACH))
        held = [total[i, j] for i, j in places]
        for k, (i, j) in enumerate(places):
            total[i, j] = held[k] + terms[:, k * points : (k + 1) * points]

    @pl.loop(0, tile_rows)
    def _(r):
        for copy in loads(r):
            copy.wait()
        for index, c in enumerate(outer_cols):
            terms = lax.dot_general(
                white[r, index], weights[r, index], ACROSS, preferred_element_type=jnp.float32
            )
            add(r, c, terms)
        for index, c in enumerate(inner_cols):
            add(r, c, spreads[r, index])

        emit_halo(r)

        @pl.when(r >= REACH)
        def _():
            emit_own(r - REACH)

    @pl.loop(tile_rows, tile_rows + 2 * REACH)
    def _(i):
        emit_halo(i)

        @pl.when(i < tile_rows + REACH)
        def _():
            emit_own(i - REACH)

    @pl.loop(0, tile_rows + 2 * REACH)
    def _(i):
        halo_copy(i).wait()

    @pl.loop(0, tile_rows)
    def _(i):
        own_copy(i).wait()


def exchange_kernel(
    halo, own, out, landed_up, landed_down, landed_left, landed_right, edges, corners, own_sem, edge_sem, send_sem, recv_sem
):
    tile_rows, tile_cols = own.shape[:2]
    inside, device = neighbourhood()
    sends = (send_sem, recv_sem)
    middle = (REACH, tile_rows - 2 * REACH)

    def place(side):
        return 0 if side[0] + side[1] < 0 else 1

    def row_copies(side):
        return [
            transfer(
                at_region(halo, outer_edge(side[0], tile_rows), (REACH, tile_cols)),
                landed_down if side[0] < 0 else landed_up,
                *sends, place(side), device, side,
            )
        ]

    def corner_copies(side):
        return [
            transfer(
                at_region(halo, outer_edge(side[0], tile_rows), outer_edge(col_side[1], tile_cols)),
                corners.at[place(opposite(side)), place(col_side)],
                *sends, 2 + place(side) + 2 * place(col_side), device, side,
            )
            for col_side in COL_SIDES
        ]

    def col_landing(side):
        return landed_right if side[1] < 0 else landed_left

    def col_middle(side):
        return [
            transfer(
                at_region(halo, (middle[0] + REACH, middle[1]), outer_edge(side[1], tile_cols)),
                col_landing(side).at[pl.ds(*middle)],
                *sends, 6 + place(side), device, side,
            )
        ]

    def col_end(side, row_side):
        return transfer(
            edges.at[place(row_side), place(side)],
            col_landing(side).at[pl.ds(*own_edge(row_side[0], tile_rows))],
            *sends, 8 + place(side) + 2 * place(row_side), device, side,
        )

    def col_ends(side):
        return [col_end(side, row_side) for row_side in ROW_SIDES]

    def edge_copy(row_side, side):
        start, count = own_edge(row_side[0], tile_rows)
        return pltpu.make_async_copy(
            at_region(halo, (start + REACH, count), outer_edge(side[1], tile_cols)),
            edges.at[place(row_side), place(side)],
            edge_sem.at[place(row_side) + 2 * place(side)],
        )

    own_copy = pltpu.make_async_copy(own, out, own_sem)
    for row_side in ROW_SIDES:
        for side in COL_SIDES:
            edge_copy(row_side, side).start()
    own_copy.start()
    greet(inside, device)
    for side in ROW_SIDES:
        start_if(inside, side, lambda: corner_copies(side))
    for side in COL_SIDES:
        start_if(inside, side, lambda: col_middle(side))
    for side in ROW_SIDES:
        start_if(inside, side, lambda: row_copies(side))
    for row_side in ROW_SIDES:
        row = place(row_side)
        wait_recv_if(inside, opposite(row_side), lambda: corner_copies(opposite(row_side)))
        for side in COL_SIDES:
            col = place(side)
            edge_copy(row_side, side).wait()

            @pl.when(inside(row_side))
            def _():
                for i in range(REACH):
                    for j in range(REACH):
                        term = corners[row, col, i, j].astype(jnp.float32)
                        value = edges[row, col, i, j].astype(jnp.float32) + term
                        edges[row, col, i, j] = value.astype(edges.dtype)

            @pl.when(inside(side))
            def _():
                col_end(side, row_side).start()

    def take(landed, side):
        row_start, row_count = own_edge(side[0], tile_rows)
        col_start, col_count = own_edge(side[1], tile_cols)

        @pl.when(inside(side))
        def _():
            @pl.loop(0, row_count)
            def _(i):
                for j in range(col_count):
                    out[row_start + i, col_start + j] += landed[i, j].astype(jnp.float32)

    own_copy.wait()
    for side, landed in zip(ROW_SIDES, (landed_up, landed_down)):
        wait_recv_if(inside, opposite(side), lambda: row_copies(opposite(side)))
        take(landed, side)
    for side, landed in zip(COL_SIDES, (landed_left, landed_right)):
        back = opposite(side)
        wait_recv_if(inside, back, lambda: col_middle(back) + col_ends(back))
        take(landed, side)
    for side in ROW_SIDES:
        wait_send_if(inside, side, lambda: row_copies(side) + corner_copies(side))
    for side in COL_SIDES:
        wait_send_if(inside, side, lambda: col_middle(side) + col_ends(side))


def shards(rhs_blocks, diag_factor, cond_factor, cond):
    tile_rows, tile_cols, count_rhs, points = rhs_blocks.shape
    conds = cond.shape[2]
    depth = conds * points
    far = cond_factor.reshape(tile_rows, tile_cols, depth, points)
    codes = jnp.transpose(cond, (2, 0, 1))
    block = (count_rhs, points)
    padded = (tile_rows + 2 * REACH, tile_cols + 2 * REACH) + block
    outer = 2 * REACH
    inner = tile_cols - outer
    spread_shape = (tile_rows, inner, count_rhs, depth + points)
    anywhere = pl.BlockSpec(memory_space=pltpu.HBM)
    scalars = pl.BlockSpec(memory_space=pltpu.SMEM)
    whole = pl.BlockSpec(memory_space=pltpu.VMEM)
    transfers = 12
    white, spread = pl.pallas_call(
        forward_kernel,
        out_shape=(
            jax.ShapeDtypeStruct((tile_rows, outer) + block, jnp.bfloat16),
            jax.ShapeDtypeStruct(spread_shape, jnp.float32),
        ),
        in_specs=[anywhere, anywhere, anywhere, scalars],
        out_specs=(whole, anywhere),
        scratch_shapes=[
            pltpu.VMEM(rhs_blocks.shape, rhs_blocks.dtype),
            pltpu.VMEM((tile_rows + 2 * REACH, tile_cols) + block, rhs_blocks.dtype),
            pltpu.VMEM(padded, rhs_blocks.dtype),
            pltpu.VMEM((tile_rows, tile_cols, depth + points, points), far.dtype),
            pltpu.VMEM(spread_shape, jnp.float32),
            pltpu.SemaphoreType.DMA((tile_rows,)),
            pltpu.SemaphoreType.DMA((tile_rows, 2)),
            pltpu.SemaphoreType.DMA((3,)),
            pltpu.SemaphoreType.DMA((transfers,)),
            pltpu.SemaphoreType.DMA((transfers,)),
        ],
        compiler_params=pltpu.CompilerParams(
            collective_id=0, has_side_effects=True, vmem_limit_bytes=63 * 2**20
        ),
        name="forward",
    )(rhs_blocks, diag_factor, far, codes)

    own, halo = pl.pallas_call(
        backward_kernel,
        out_shape=(
            jax.ShapeDtypeStruct(rhs_blocks.shape, jnp.float32),
            jax.ShapeDtypeStruct(padded, jnp.bfloat16),
        ),
        in_specs=[whole, anywhere, anywhere, anywhere, scalars],
        out_specs=(anywhere, anywhere),
        scratch_shapes=[
            pltpu.VMEM((tile_rows, outer, depth + points, points), far.dtype),
            pltpu.VMEM(spread_shape, jnp.float32),
            pltpu.VMEM(padded, jnp.float32),
            pltpu.VMEM(rhs_blocks.shape, jnp.float32),
            pltpu.VMEM(padded, jnp.bfloat16),
            pltpu.SemaphoreType.DMA((tile_rows, 5)),
            pltpu.SemaphoreType.DMA((tile_rows,)),
            pltpu.SemaphoreType.DMA((tile_rows + 2 * REACH,)),
        ],
        compiler_params=pltpu.CompilerParams(vmem_limit_bytes=63 * 2**20),
        name="backward",
    )(white, diag_factor, far, spread, codes)

    row_part = pltpu.VMEM((REACH, tile_cols) + block, jnp.bfloat16)
    col_part = pltpu.VMEM((tile_rows, REACH) + block, jnp.bfloat16)
    return pl.pallas_call(
        exchange_kernel,
        out_shape=jax.ShapeDtypeStruct(rhs_blocks.shape, jnp.float32),
        in_specs=[anywhere, anywhere],
        out_specs=whole,
        scratch_shapes=[
            row_part,
            row_part,
            col_part,
            col_part,
            pltpu.VMEM((2, 2, REACH, REACH) + block, jnp.bfloat16),
            pltpu.VMEM((2, 2, REACH, REACH) + block, jnp.bfloat16),
            pltpu.SemaphoreType.DMA,
            pltpu.SemaphoreType.DMA((4,)),
            pltpu.SemaphoreType.DMA((transfers,)),
            pltpu.SemaphoreType.DMA((transfers,)),
        ],
        compiler_params=pltpu.CompilerParams(
            collective_id=1, has_side_effects=True, vmem_limit_bytes=61 * 2**20
        ),
        name="exchange",
    )(halo, own)


def solution(mesh):
    in_specs = (
        P("gx", "gy", None, None),
        P("gx", "gy", None, None),
        P("gx", "gy", None, None, None),
        P("gx", "gy", None),
    )
    out_specs = P("gx", "gy", None, None)
    return jax.shard_map(shards, mesh=mesh, in_specs=in_specs, out_specs=out_specs, check_vma=False)
```

```python
import functools

import jax
import jax.numpy as jnp
from jax import lax
from jax.experimental import pallas as pl
from jax.experimental.pallas import tpu as pltpu
from jax.sharding import PartitionSpec as P

MESH = pl.DeviceIdType.MESH
REACH = 2
SPAN = 2 * REACH + 1
ACROSS = (((1,), (1,)), ((), ()))
ROW_SIDES = [(-1, 0), (1, 0)]
COL_SIDES = [(0, -1), (0, 1)]
SIDES = ROW_SIDES + COL_SIDES


def own_edge(step, size):
    return {-1: (0, REACH), 0: (0, size), 1: (size - REACH, REACH)}[step]


def outer_edge(step, size):
    return {-1: (0, REACH), 0: (REACH, size), 1: (REACH + size, REACH)}[step]


def at_region(ref, row_part, col_part):
    return ref.at[pl.ds(*row_part), pl.ds(*col_part)]


def neighbourhood():
    row, col = lax.axis_index("gx"), lax.axis_index("gy")
    rows, cols = lax.axis_size("gx"), lax.axis_size("gy")

    def inside(side):
        r, c = row + side[0], col + side[1]
        return (r >= 0) & (r < rows) & (c >= 0) & (c < cols)

    def device(side):
        return {"gx": row + side[0], "gy": col + side[1]}

    return inside, device


def greet(inside, device):
    barrier = pltpu.get_barrier_semaphore()
    count = jnp.int32(0)
    for side in SIDES:
        count = count + inside(side).astype(jnp.int32)

        @pl.when(inside(side))
        def _():
            pl.semaphore_signal(barrier, inc=1, device_id=device(side), device_id_type=MESH)

    pl.semaphore_wait(barrier, count)


def opposite(side):
    return (-side[0], -side[1])


def transfer(src, dst, send_sem, recv_sem, index, device, side):
    return pltpu.make_async_remote_copy(
        src_ref=src,
        dst_ref=dst,
        send_sem=send_sem.at[index],
        recv_sem=recv_sem.at[index],
        device_id=device(side),
        device_id_type=MESH,
    )


def start_if(inside, side, copies):
    @pl.when(inside(side))
    def _():
        for copy in copies():
            copy.start()


def wait_recv_if(inside, side, copies):
    @pl.when(inside(opposite(side)))
    def _():
        for copy in copies():
            copy.wait_recv()


def wait_send_if(inside, side, copies):
    @pl.when(inside(side))
    def _():
        for copy in copies():
            copy.wait_send()


def forward_kernel(
    rhs, diag, far, cond, white, spread_out, local, rowed, wide, padded, weights, spread, spread_sem, load_sem, rhs_sem, send_sem, recv_sem
):
    tile_rows, tile_cols, count_rhs, points = rhs.shape
    depth = far.shape[2]
    inside, device = neighbourhood()
    row_order = list(range(REACH, tile_rows - REACH))
    row_order += [r for r in range(tile_rows) if r not in row_order]
    sends = (send_sem, recv_sem)
    middle = (REACH, tile_rows - 2 * REACH)

    def loads(r):
        return [
            pltpu.make_async_copy(far.at[r], weights.at[r, :, pl.ds(0, depth)], load_sem.at[r, 0]),
            pltpu.make_async_copy(diag.at[r], weights.at[r, :, pl.ds(depth, points)], load_sem.at[r, 1]),
        ]

    local_copy = pltpu.make_async_copy(rhs, local, rhs_sem.at[0])
    centre_copy = pltpu.make_async_copy(rhs, rowed.at[pl.ds(REACH, tile_rows)], rhs_sem.at[1])
    padded_copy = pltpu.make_async_copy(
        rowed, padded.at[:, pl.ds(REACH, tile_cols)], rhs_sem.at[2]
    )
    wide_copy = pltpu.make_async_copy(rhs, wide.at[:, pl.ds(REACH, tile_cols)], rhs_sem.at[3])

    def side_copy(side):
        cols = pl.ds(*outer_edge(side[1], tile_cols))
        return pltpu.make_async_copy(
            wide.at[:, cols],
            padded.at[pl.ds(REACH, tile_rows), cols],
            rhs_sem.at[4 + (0 if side[1] < 0 else 1)],
        )

    def row_copies(side):
        return [
            transfer(
                rhs.at[pl.ds(*own_edge(side[0], tile_rows))],
                rowed.at[pl.ds(*outer_edge(-side[0], tile_rows))],
                *sends, 0 if side[0] < 0 else 1, device, side,
            )
        ]

    def col_copy(side, part, index):
        return transfer(
            at_region(rhs, part, own_edge(side[1], tile_cols)),
            at_region(wide, part, outer_edge(-side[1], tile_cols)),
            *sends, index + (0 if side[1] < 0 else 1), device, side,
        )

    def col_ends(side):
        return [
            col_copy(side, own_edge(-1, tile_rows), 2),
            col_copy(side, own_edge(1, tile_rows), 4),
        ]

    def col_middle(side):
        return [col_copy(side, middle, 6)]

    def corner_copy(side, col_side):
        start, count = own_edge(side[0], tile_rows)
        cols = outer_edge(col_side[1], tile_cols)
        return transfer(
            at_region(wide, (start, count), cols),
            at_region(padded, outer_edge(-side[0], tile_rows), cols),
            *sends,
            8 + (0 if side[0] < 0 else 1) + (0 if col_side[1] < 0 else 2),
            device, side,
        )

    local_copy.start()
    for copy in loads(row_order[0]):
        copy.start()
    greet(inside, device)
    for side in COL_SIDES:
        start_if(inside, side, lambda: col_ends(side))
    for side in COL_SIDES:
        start_if(inside, side, lambda: col_middle(side))
    for side in ROW_SIDES:
        start_if(inside, side, lambda: row_copies(side))
    centre_copy.start()
    wide_copy.start()
    for r in row_order[1:]:
        for copy in loads(r):
            copy.start()

    def mix(source, row_shift, col_shift, r, c):
        parts = []
        for k in range(depth // points):
            code = cond[k, r, c]
            parts.append(source[r + code // SPAN + row_shift, c + lax.rem(code, SPAN) + col_shift])
        parts.append(source[r + REACH + row_shift, c + REACH + col_shift])
        mixed = jnp.dot(
            jnp.concatenate(parts, axis=1), weights[r, c], preferred_element_type=jnp.float32
        )
        return mixed.astype(white.dtype)

    def spread_copy(r):
        return pltpu.make_async_copy(spread.at[r], spread_out.at[r], spread_sem.at[r])

    def inner_row(source, row_shift, r):
        for index, c in enumerate(inner_cols):
            value = mix(source, row_shift, -REACH, r, c)
            spread[r, index] = lax.dot_general(
                value, weights[r, c], ACROSS, preferred_element_type=jnp.float32
            )
        spread_copy(r).start()

    inner_cols = list(range(REACH, tile_cols - REACH))
    outer_cols = [c for c in range(tile_cols) if c not in inner_cols]

    local_copy.wait()
    for r in range(REACH, tile_rows - REACH):
        for copy in loads(r):
            copy.wait()

    @pl.loop(REACH, tile_rows - REACH)
    def _(r):
        inner_row(local, -REACH, r)

    centre_copy.wait()
    for side in ROW_SIDES:
        wait_recv_if(inside, side, lambda: row_copies(side))
    padded_copy.start()

    for col_side in COL_SIDES:
        wait_recv_if(inside, opposite(col_side), lambda: col_ends(opposite(col_side)))
        for side in ROW_SIDES:

            @pl.when(inside(side) & inside(col_side))
            def _():
                corner_copy(side, col_side).start()

    for r in range(tile_rows):
        if r < REACH or r >= tile_rows - REACH:
            for copy in loads(r):
                copy.wait()

    @pl.loop(0, 2 * REACH)
    def _(step):
        r = jnp.where(step < REACH, step, tile_rows - 2 * REACH + step)
        inner_row(rowed, 0, r)

    def outer_row(source, row_shift, r):
        for index, c in enumerate(outer_cols):
            white[r, index] = mix(source, row_shift, 0, r, c)
        spread_copy(r).wait()

    wide_copy.wait()
    for side in COL_SIDES:
        wait_recv_if(inside, side, lambda: col_middle(side))
    for side in COL_SIDES:
        side_copy(side).start()

    @pl.loop(REACH, tile_rows - REACH)
    def _(r):
        outer_row(wide, -REACH, r)

    padded_copy.wait()
    for side in COL_SIDES:
        side_copy(side).wait()
    for col_side in COL_SIDES:
        for side in ROW_SIDES:

            @pl.when(inside(opposite(side)) & inside(col_side))
            def _():
                corner_copy(side, col_side).wait_recv()

    @pl.loop(0, 2 * REACH)
    def _(step):
        outer_row(padded, 0, jnp.where(step < REACH, step, tile_rows - 2 * REACH + step))

    for side in COL_SIDES:
        wait_send_if(inside, side, lambda: col_ends(side) + col_middle(side))
    for side in ROW_SIDES:
        wait_send_if(inside, side, lambda: row_copies(side))
        for col_side in COL_SIDES:

            @pl.when(inside(side) & inside(col_side))
            def _():
                corner_copy(side, col_side).wait_send()


def backward_kernel(
    white, diag, far, spread, cond, own, halo, weights, spreads, total, own_out, halo_out, load_sem, own_sem, halo_sem
):
    tile_rows, tile_cols, points = diag.shape[:3]
    depth = far.shape[2]
    conds = depth // points
    inner_cols = list(range(REACH, tile_cols - REACH))
    outer_cols = [c for c in range(tile_cols) if c not in inner_cols]

    def loads(r):
        copies = [pltpu.make_async_copy(spread.at[r], spreads.at[r], load_sem.at[r, 0])]
        for index, side in enumerate(COL_SIDES):
            cols = pl.ds(*own_edge(side[1], tile_cols))
            slots = pl.ds(index * REACH, REACH)
            copies += [
                pltpu.make_async_copy(
                    far.at[r, cols], weights.at[r, slots, pl.ds(0, depth)], load_sem.at[r, 1 + 2 * index]
                ),
                pltpu.make_async_copy(
                    diag.at[r, cols], weights.at[r, slots, pl.ds(depth, points)], load_sem.at[r, 2 + 2 * index]
                ),
            ]
        return copies

    @pl.loop(0, tile_rows)
    def _(r):
        for copy in loads(r):
            copy.start()

    @pl.loop(0, tile_rows + 2 * REACH)
    def _(i):
        total[i] = jnp.zeros(total.shape[1:], jnp.float32)

    def halo_copy(i):
        return pltpu.make_async_copy(halo_out.at[i], halo.at[i], halo_sem.at[i])

    def own_copy(i):
        return pltpu.make_async_copy(own_out.at[i], own.at[i], own_sem.at[i])

    def emit_halo(i):
        for j in range(tile_cols + 2 * REACH):
            halo_out[i, j] = total[i, j].astype(halo.dtype)
        halo_copy(i).start()

    def emit_own(i):
        for j in range(tile_cols):
            own_out[i, j] = total[i + REACH, j + REACH]
        own_copy(i).start()

    def add(r, c, terms):
        places = []
        for k in range(conds):
            code = cond[k, r, c]
            places.append((r + code // SPAN, c + lax.rem(code, SPAN)))
        places.append((r + REACH, c + REACH))
        held = [total[i, j] for i, j in places]
        for k, (i, j) in enumerate(places):
            total[i, j] = held[k] + terms[:, k * points : (k + 1) * points]

    @pl.loop(0, tile_rows)
    def _(r):
        for copy in loads(r):
            copy.wait()
        for index, c in enumerate(outer_cols):
            terms = lax.dot_general(
                white[r, index], weights[r, index], ACROSS, preferred_element_type=jnp.float32
            )
            add(r, c, terms)
        for index, c in enumerate(inner_cols):
            add(r, c, spreads[r, index])

        emit_halo(r)

        @pl.when(r >= REACH)
        def _():
            emit_own(r - REACH)

    @pl.loop(tile_rows, tile_rows + 2 * REACH)
    def _(i):
        emit_halo(i)

        @pl.when(i < tile_rows + REACH)
        def _():
            emit_own(i - REACH)

    @pl.loop(0, tile_rows + 2 * REACH)
    def _(i):
        halo_copy(i).wait()

    @pl.loop(0, tile_rows)
    def _(i):
        own_copy(i).wait()


def exchange_kernel(halo, landed_up, landed_down, landed_left, landed_right, edges, corners, edge_sem, send_sem, recv_sem):
    tile_rows, tile_cols = landed_left.shape[0], landed_up.shape[1]
    inside, device = neighbourhood()
    sends = (send_sem, recv_sem)
    middle = (REACH, tile_rows - 2 * REACH)

    def place(side):
        return 0 if side[0] + side[1] < 0 else 1

    def row_copies(side):
        return [
            transfer(
                at_region(halo, outer_edge(side[0], tile_rows), (REACH, tile_cols)),
                landed_down if side[0] < 0 else landed_up,
                *sends, place(side), device, side,
            )
        ]

    def corner_copies(side):
        return [
            transfer(
                at_region(halo, outer_edge(side[0], tile_rows), outer_edge(col_side[1], tile_cols)),
                corners.at[place(opposite(side)), place(col_side)],
                *sends, 2 + place(side) + 2 * place(col_side), device, side,
            )
            for col_side in COL_SIDES
        ]

    def col_landing(side):
        return landed_right if side[1] < 0 else landed_left

    def col_middle(side):
        return [
            transfer(
                at_region(halo, (middle[0] + REACH, middle[1]), outer_edge(side[1], tile_cols)),
                col_landing(side).at[pl.ds(*middle)],
                *sends, 6 + place(side), device, side,
            )
        ]

    def col_end(side, row_side):
        return transfer(
            edges.at[place(row_side), place(side)],
            col_landing(side).at[pl.ds(*own_edge(row_side[0], tile_rows))],
            *sends, 8 + place(side) + 2 * place(row_side), device, side,
        )

    def col_ends(side):
        return [col_end(side, row_side) for row_side in ROW_SIDES]

    def edge_copy(row_side, side):
        start, count = own_edge(row_side[0], tile_rows)
        return pltpu.make_async_copy(
            at_region(halo, (start + REACH, count), outer_edge(side[1], tile_cols)),
            edges.at[place(row_side), place(side)],
            edge_sem.at[place(row_side) + 2 * place(side)],
        )

    for row_side in ROW_SIDES:
        for side in COL_SIDES:
            edge_copy(row_side, side).start()
    greet(inside, device)
    for side in ROW_SIDES:
        start_if(inside, side, lambda: corner_copies(side))
    for side in COL_SIDES:
        start_if(inside, side, lambda: col_middle(side))
    for side in ROW_SIDES:
        start_if(inside, side, lambda: row_copies(side))
    for row_side in ROW_SIDES:
        row = place(row_side)
        wait_recv_if(inside, opposite(row_side), lambda: corner_copies(opposite(row_side)))
        for side in COL_SIDES:
            col = place(side)
            edge_copy(row_side, side).wait()

            @pl.when(inside(row_side))
            def _():
                for i in range(REACH):
                    for j in range(REACH):
                        term = corners[row, col, i, j].astype(jnp.float32)
                        value = edges[row, col, i, j].astype(jnp.float32) + term
                        edges[row, col, i, j] = value.astype(edges.dtype)

            @pl.when(inside(side))
            def _():
                col_end(side, row_side).start()

    for side in ROW_SIDES:
        wait_recv_if(inside, side, lambda: row_copies(side))
        wait_send_if(inside, side, lambda: row_copies(side) + corner_copies(side))
    for side in COL_SIDES:
        wait_recv_if(inside, side, lambda: col_middle(side) + col_ends(side))
        wait_send_if(inside, side, lambda: col_middle(side) + col_ends(side))


def finish_kernel(own, *refs):
    landed, out, held, parts = refs[:4], refs[4], refs[5], refs[6:10]
    part_sem, load_sem, store_sem = refs[10:]
    landed_up, landed_down, landed_left, landed_right = parts
    tile_rows, tile_cols = own.shape[:2]
    inside, _ = neighbourhood()

    def load(i):
        return pltpu.make_async_copy(own.at[i], held.at[i], load_sem.at[i])

    def store(i):
        return pltpu.make_async_copy(held.at[i], out.at[i], store_sem.at[i])

    def fetch(index):
        return pltpu.make_async_copy(landed[index], parts[index], part_sem.at[index])

    load(0).start()
    for index in range(4):
        fetch(index).start()
    for i in range(1, tile_rows):
        load(i).start()
    for index in range(4):
        fetch(index).wait()
    for i in range(tile_rows):
        load(i).wait()
        for side, part in zip(COL_SIDES, (landed_left, landed_right)):
            start, count = own_edge(side[1], tile_cols)

            @pl.when(inside(side))
            def _():
                held[i, pl.ds(start, count)] += part[i].astype(jnp.float32)

        for side, part in zip(ROW_SIDES, (landed_up, landed_down)):
            start, count = own_edge(side[0], tile_rows)
            if start <= i < start + count:

                @pl.when(inside(side))
                def _():
                    held[i] += part[i - start].astype(jnp.float32)

        store(i).start()
    for i in range(tile_rows):
        store(i).wait()


def shards(rhs_blocks, diag_factor, cond_factor, cond):
    tile_rows, tile_cols, count_rhs, points = rhs_blocks.shape
    conds = cond.shape[2]
    depth = conds * points
    far = cond_factor.reshape(tile_rows, tile_cols, depth, points)
    codes = jnp.transpose(cond, (2, 0, 1))
    block = (count_rhs, points)
    padded = (tile_rows + 2 * REACH, tile_cols + 2 * REACH) + block
    outer = 2 * REACH
    inner = tile_cols - outer
    spread_shape = (tile_rows, inner, count_rhs, depth + points)
    anywhere = pl.BlockSpec(memory_space=pltpu.HBM)
    scalars = pl.BlockSpec(memory_space=pltpu.SMEM)
    whole = pl.BlockSpec(memory_space=pltpu.VMEM)
    transfers = 12
    white, spread = pl.pallas_call(
        forward_kernel,
        out_shape=(
            jax.ShapeDtypeStruct((tile_rows, outer) + block, jnp.bfloat16),
            jax.ShapeDtypeStruct(spread_shape, jnp.float32),
        ),
        in_specs=[anywhere, anywhere, anywhere, scalars],
        out_specs=(whole, anywhere),
        scratch_shapes=[
            pltpu.VMEM(rhs_blocks.shape, rhs_blocks.dtype),
            pltpu.VMEM((tile_rows + 2 * REACH, tile_cols) + block, rhs_blocks.dtype),
            pltpu.VMEM((tile_rows, tile_cols + 2 * REACH) + block, rhs_blocks.dtype),
            pltpu.VMEM(padded, rhs_blocks.dtype),
            pltpu.VMEM((tile_rows, tile_cols, depth + points, points), far.dtype),
            pltpu.VMEM(spread_shape, jnp.float32),
            pltpu.SemaphoreType.DMA((tile_rows,)),
            pltpu.SemaphoreType.DMA((tile_rows, 2)),
            pltpu.SemaphoreType.DMA((6,)),
            pltpu.SemaphoreType.DMA((transfers,)),
            pltpu.SemaphoreType.DMA((transfers,)),
        ],
        compiler_params=pltpu.CompilerParams(
            collective_id=0, has_side_effects=True, vmem_limit_bytes=63 * 2**20
        ),
        name="forward",
    )(rhs_blocks, diag_factor, far, codes)

    own, halo = pl.pallas_call(
        backward_kernel,
        out_shape=(
            jax.ShapeDtypeStruct(rhs_blocks.shape, jnp.float32),
            jax.ShapeDtypeStruct(padded, jnp.bfloat16),
        ),
        in_specs=[whole, anywhere, anywhere, anywhere, scalars],
        out_specs=(anywhere, anywhere),
        scratch_shapes=[
            pltpu.VMEM((tile_rows, outer, depth + points, points), far.dtype),
            pltpu.VMEM(spread_shape, jnp.float32),
            pltpu.VMEM(padded, jnp.float32),
            pltpu.VMEM(rhs_blocks.shape, jnp.float32),
            pltpu.VMEM(padded, jnp.bfloat16),
            pltpu.SemaphoreType.DMA((tile_rows, 5)),
            pltpu.SemaphoreType.DMA((tile_rows,)),
            pltpu.SemaphoreType.DMA((tile_rows + 2 * REACH,)),
        ],
        compiler_params=pltpu.CompilerParams(vmem_limit_bytes=63 * 2**20),
        name="backward",
    )(white, diag_factor, far, spread, codes)

    row_part = jax.ShapeDtypeStruct((REACH, tile_cols) + block, jnp.bfloat16)
    col_part = jax.ShapeDtypeStruct((tile_rows, REACH) + block, jnp.bfloat16)
    landed = pl.pallas_call(
        exchange_kernel,
        out_shape=(row_part, row_part, col_part, col_part),
        in_specs=[anywhere],
        out_specs=(anywhere,) * 4,
        scratch_shapes=[
            pltpu.VMEM((2, 2, REACH, REACH) + block, jnp.bfloat16),
            pltpu.VMEM((2, 2, REACH, REACH) + block, jnp.bfloat16),
            pltpu.SemaphoreType.DMA((4,)),
            pltpu.SemaphoreType.DMA((transfers,)),
            pltpu.SemaphoreType.DMA((transfers,)),
        ],
        compiler_params=pltpu.CompilerParams(
            collective_id=1, has_side_effects=True, vmem_limit_bytes=63 * 2**20
        ),
        name="exchange",
    )(halo)

    return pl.pallas_call(
        finish_kernel,
        out_shape=jax.ShapeDtypeStruct(rhs_blocks.shape, jnp.float32),
        in_specs=[anywhere] * 5,
        out_specs=anywhere,
        scratch_shapes=[
            pltpu.VMEM(rhs_blocks.shape, jnp.float32),
            pltpu.VMEM(row_part.shape, row_part.dtype),
            pltpu.VMEM(row_part.shape, row_part.dtype),
            pltpu.VMEM(col_part.shape, col_part.dtype),
            pltpu.VMEM(col_part.shape, col_part.dtype),
            pltpu.SemaphoreType.DMA((4,)),
            pltpu.SemaphoreType.DMA((tile_rows,)),
            pltpu.SemaphoreType.DMA((tile_rows,)),
        ],
        compiler_params=pltpu.CompilerParams(vmem_limit_bytes=63 * 2**20),
        name="finish",
    )(own, *landed)


def solution(mesh):
    in_specs = (
        P("gx", "gy", None, None),
        P("gx", "gy", None, None),
        P("gx", "gy", None, None, None),
        P("gx", "gy", None),
    )
    out_specs = P("gx", "gy", None, None)
    return jax.shard_map(shards, mesh=mesh, in_specs=in_specs, out_specs=out_specs, check_vma=False)
```

```python
import functools

import jax
import jax.numpy as jnp
from jax import lax
from jax.experimental import pallas as pl
from jax.experimental.pallas import tpu as pltpu
from jax.sharding import PartitionSpec as P

MESH = pl.DeviceIdType.MESH
REACH = 2
SPAN = 2 * REACH + 1
ACROSS = (((1,), (1,)), ((), ()))
ROW_SIDES = [(-1, 0), (1, 0)]
COL_SIDES = [(0, -1), (0, 1)]
SIDES = ROW_SIDES + COL_SIDES


def offsets(code):
    off_row = (code * 13) >> 6
    return off_row, code - off_row * SPAN


def own_edge(step, size):
    return {-1: (0, REACH), 0: (0, size), 1: (size - REACH, REACH)}[step]


def outer_edge(step, size):
    return {-1: (0, REACH), 0: (REACH, size), 1: (REACH + size, REACH)}[step]


def at_region(ref, row_part, col_part):
    return ref.at[pl.ds(*row_part), pl.ds(*col_part)]


def neighbourhood():
    row, col = lax.axis_index("gx"), lax.axis_index("gy")
    rows, cols = lax.axis_size("gx"), lax.axis_size("gy")

    def inside(side):
        r, c = row + side[0], col + side[1]
        return (r >= 0) & (r < rows) & (c >= 0) & (c < cols)

    def device(side):
        return {"gx": row + side[0], "gy": col + side[1]}

    return inside, device


def greet(inside, device):
    barrier = pltpu.get_barrier_semaphore()
    count = jnp.int32(0)
    for side in SIDES:
        count = count + inside(side).astype(jnp.int32)

        @pl.when(inside(side))
        def _():
            pl.semaphore_signal(barrier, inc=1, device_id=device(side), device_id_type=MESH)

    pl.semaphore_wait(barrier, count)


def opposite(side):
    return (-side[0], -side[1])


def transfer(src, dst, send_sem, recv_sem, index, device, side):
    return pltpu.make_async_remote_copy(
        src_ref=src,
        dst_ref=dst,
        send_sem=send_sem.at[index],
        recv_sem=recv_sem.at[index],
        device_id=device(side),
        device_id_type=MESH,
    )


def start_if(inside, side, copies):
    @pl.when(inside(side))
    def _():
        for copy in copies():
            copy.start()


def wait_recv_if(inside, side, copies):
    @pl.when(inside(opposite(side)))
    def _():
        for copy in copies():
            copy.wait_recv()


def wait_send_if(inside, side, copies):
    @pl.when(inside(side))
    def _():
        for copy in copies():
            copy.wait_send()


def forward_kernel(
    rhs, diag, far, cond, white, spread_out, local, rowed, wide, padded, weights, spread, spread_sem, load_sem, rhs_sem, send_sem, recv_sem
):
    tile_rows, tile_cols, count_rhs, points = rhs.shape
    depth = far.shape[2]
    inside, device = neighbourhood()
    row_order = list(range(REACH, tile_rows - REACH))
    row_order += [r for r in range(tile_rows) if r not in row_order]
    sends = (send_sem, recv_sem)
    middle = (REACH, tile_rows - 2 * REACH)

    def loads(r):
        return [
            pltpu.make_async_copy(far.at[r], weights.at[r, :, pl.ds(0, depth)], load_sem.at[r, 0]),
            pltpu.make_async_copy(diag.at[r], weights.at[r, :, pl.ds(depth, points)], load_sem.at[r, 1]),
        ]

    local_copy = pltpu.make_async_copy(rhs, local, rhs_sem.at[0])
    centre_copy = pltpu.make_async_copy(rhs, rowed.at[pl.ds(REACH, tile_rows)], rhs_sem.at[1])
    padded_copy = pltpu.make_async_copy(
        rowed, padded.at[:, pl.ds(REACH, tile_cols)], rhs_sem.at[2]
    )
    wide_copy = pltpu.make_async_copy(rhs, wide.at[:, pl.ds(REACH, tile_cols)], rhs_sem.at[3])

    def side_copy(side):
        cols = pl.ds(*outer_edge(side[1], tile_cols))
        return pltpu.make_async_copy(
            wide.at[:, cols],
            padded.at[pl.ds(REACH, tile_rows), cols],
            rhs_sem.at[4 + (0 if side[1] < 0 else 1)],
        )

    def row_copies(side):
        return [
            transfer(
                rhs.at[pl.ds(*own_edge(side[0], tile_rows))],
                rowed.at[pl.ds(*outer_edge(-side[0], tile_rows))],
                *sends, 0 if side[0] < 0 else 1, device, side,
            )
        ]

    def col_copy(side, part, index):
        return transfer(
            at_region(rhs, part, own_edge(side[1], tile_cols)),
            at_region(wide, part, outer_edge(-side[1], tile_cols)),
            *sends, index + (0 if side[1] < 0 else 1), device, side,
        )

    def col_ends(side):
        return [
            col_copy(side, own_edge(-1, tile_rows), 2),
            col_copy(side, own_edge(1, tile_rows), 4),
        ]

    def col_middle(side):
        return [col_copy(side, middle, 6)]

    def corner_copy(side, col_side):
        start, count = own_edge(side[0], tile_rows)
        cols = outer_edge(col_side[1], tile_cols)
        return transfer(
            at_region(wide, (start, count), cols),
            at_region(padded, outer_edge(-side[0], tile_rows), cols),
            *sends,
            8 + (0 if side[0] < 0 else 1) + (0 if col_side[1] < 0 else 2),
            device, side,
        )

    local_copy.start()
    for copy in loads(row_order[0]):
        copy.start()
    greet(inside, device)
    for side in COL_SIDES:
        start_if(inside, side, lambda: col_ends(side))
    for side in COL_SIDES:
        start_if(inside, side, lambda: col_middle(side))
    for side in ROW_SIDES:
        start_if(inside, side, lambda: row_copies(side))
    centre_copy.start()
    wide_copy.start()
    for r in row_order[1:]:
        for copy in loads(r):
            copy.start()

    def mix(source, row_shift, col_shift, r, c):
        parts = []
        for k in range(depth // points):
            off_row, off_col = offsets(cond[k, r, c])
            parts.append(source[r + off_row + row_shift, c + off_col + col_shift])
        parts.append(source[r + REACH + row_shift, c + REACH + col_shift])
        mixed = jnp.dot(
            jnp.concatenate(parts, axis=1), weights[r, c], preferred_element_type=jnp.float32
        )
        return mixed.astype(white.dtype)

    def spread_copy(r):
        return pltpu.make_async_copy(spread.at[r], spread_out.at[r], spread_sem.at[r])

    def inner_row(source, row_shift, r):
        for index, c in enumerate(inner_cols):
            value = mix(source, row_shift, -REACH, r, c)
            spread[r, index] = lax.dot_general(
                value, weights[r, c], ACROSS, preferred_element_type=jnp.float32
            )
        spread_copy(r).start()

    inner_cols = list(range(REACH, tile_cols - REACH))
    outer_cols = [c for c in range(tile_cols) if c not in inner_cols]

    local_copy.wait()
    for r in range(REACH, tile_rows - REACH):
        for copy in loads(r):
            copy.wait()

    @pl.loop(REACH, tile_rows - REACH, unroll=2)
    def _(r):
        inner_row(local, -REACH, r)

    centre_copy.wait()
    for side in ROW_SIDES:
        wait_recv_if(inside, side, lambda: row_copies(side))
    padded_copy.start()

    for col_side in COL_SIDES:
        wait_recv_if(inside, opposite(col_side), lambda: col_ends(opposite(col_side)))
        for side in ROW_SIDES:

            @pl.when(inside(side) & inside(col_side))
            def _():
                corner_copy(side, col_side).start()

    for r in range(tile_rows):
        if r < REACH or r >= tile_rows - REACH:
            for copy in loads(r):
                copy.wait()

    @pl.loop(0, 2 * REACH, unroll=2)
    def _(step):
        r = jnp.where(step < REACH, step, tile_rows - 2 * REACH + step)
        inner_row(rowed, 0, r)

    def outer_row(source, row_shift, r):
        for index, c in enumerate(outer_cols):
            white[r, index] = mix(source, row_shift, 0, r, c)
        spread_copy(r).wait()

    wide_copy.wait()
    for side in COL_SIDES:
        wait_recv_if(inside, side, lambda: col_middle(side))
    for side in COL_SIDES:
        side_copy(side).start()

    @pl.loop(REACH, tile_rows - REACH, unroll=2)
    def _(r):
        outer_row(wide, -REACH, r)

    padded_copy.wait()
    for side in COL_SIDES:
        side_copy(side).wait()
    for col_side in COL_SIDES:
        for side in ROW_SIDES:

            @pl.when(inside(opposite(side)) & inside(col_side))
            def _():
                corner_copy(side, col_side).wait_recv()

    @pl.loop(0, 2 * REACH, unroll=2)
    def _(step):
        outer_row(padded, 0, jnp.where(step < REACH, step, tile_rows - 2 * REACH + step))

    for side in COL_SIDES:
        wait_send_if(inside, side, lambda: col_ends(side) + col_middle(side))
    for side in ROW_SIDES:
        wait_send_if(inside, side, lambda: row_copies(side))
        for col_side in COL_SIDES:

            @pl.when(inside(side) & inside(col_side))
            def _():
                corner_copy(side, col_side).wait_send()


def backward_kernel(
    white, diag, far, spread, cond, own, halo, weights, spreads, total, own_out, halo_out, load_sem, own_sem, halo_sem
):
    tile_rows, tile_cols, points = diag.shape[:3]
    depth = far.shape[2]
    conds = depth // points
    inner_cols = list(range(REACH, tile_cols - REACH))
    outer_cols = [c for c in range(tile_cols) if c not in inner_cols]

    def loads(r):
        copies = [pltpu.make_async_copy(spread.at[r], spreads.at[r], load_sem.at[r, 0])]
        for index, side in enumerate(COL_SIDES):
            cols = pl.ds(*own_edge(side[1], tile_cols))
            slots = pl.ds(index * REACH, REACH)
            copies += [
                pltpu.make_async_copy(
                    far.at[r, cols], weights.at[r, slots, pl.ds(0, depth)], load_sem.at[r, 1 + 2 * index]
                ),
                pltpu.make_async_copy(
                    diag.at[r, cols], weights.at[r, slots, pl.ds(depth, points)], load_sem.at[r, 2 + 2 * index]
                ),
            ]
        return copies

    @pl.loop(0, tile_rows)
    def _(r):
        for copy in loads(r):
            copy.start()

    @pl.loop(0, tile_rows + 2 * REACH)
    def _(i):
        total[i] = jnp.zeros(total.shape[1:], jnp.float32)

    def halo_copy(i):
        return pltpu.make_async_copy(halo_out.at[i], halo.at[i], halo_sem.at[i])

    def own_copy(i):
        return pltpu.make_async_copy(own_out.at[i], own.at[i], own_sem.at[i])

    def emit_halo(i):
        for j in range(tile_cols + 2 * REACH):
            halo_out[i, j] = total[i, j].astype(halo.dtype)
        halo_copy(i).start()

    def emit_own(i):
        for j in range(tile_cols):
            own_out[i, j] = total[i + REACH, j + REACH]
        own_copy(i).start()

    def add(r, c, terms):
        places = []
        for k in range(conds):
            off_row, off_col = offsets(cond[k, r, c])
            places.append((r + off_row, c + off_col))
        places.append((r + REACH, c + REACH))
        held = [total[i, j] for i, j in places]
        for k, (i, j) in enumerate(places):
            total[i, j] = held[k] + terms[:, k * points : (k + 1) * points]

    @pl.loop(0, tile_rows)
    def _(r):
        for copy in loads(r):
            copy.wait()
        for index, c in enumerate(outer_cols):
            terms = lax.dot_general(
                white[r, index], weights[r, index], ACROSS, preferred_element_type=jnp.float32
            )
            add(r, c, terms)
        for index, c in enumerate(inner_cols):
            add(r, c, spreads[r, index])

        emit_halo(r)

        @pl.when(r >= REACH)
        def _():
            emit_own(r - REACH)

    @pl.loop(tile_rows, tile_rows + 2 * REACH)
    def _(i):
        emit_halo(i)

        @pl.when(i < tile_rows + REACH)
        def _():
            emit_own(i - REACH)

    @pl.loop(0, tile_rows + 2 * REACH)
    def _(i):
        halo_copy(i).wait()

    @pl.loop(0, tile_rows)
    def _(i):
        own_copy(i).wait()


def exchange_kernel(halo, landed_up, landed_down, landed_left, landed_right, edges, corners, edge_sem, send_sem, recv_sem):
    tile_rows, tile_cols = landed_left.shape[0], landed_up.shape[1]
    inside, device = neighbourhood()
    sends = (send_sem, recv_sem)
    middle = (REACH, tile_rows - 2 * REACH)

    def place(side):
        return 0 if side[0] + side[1] < 0 else 1

    def row_copies(side):
        return [
            transfer(
                at_region(halo, outer_edge(side[0], tile_rows), (REACH, tile_cols)),
                landed_down if side[0] < 0 else landed_up,
                *sends, place(side), device, side,
            )
        ]

    def corner_copies(side):
        return [
            transfer(
                at_region(halo, outer_edge(side[0], tile_rows), outer_edge(col_side[1], tile_cols)),
                corners.at[place(opposite(side)), place(col_side)],
                *sends, 2 + place(side) + 2 * place(col_side), device, side,
            )
            for col_side in COL_SIDES
        ]

    def col_landing(side):
        return landed_right if side[1] < 0 else landed_left

    def col_middle(side):
        return [
            transfer(
                at_region(halo, (middle[0] + REACH, middle[1]), outer_edge(side[1], tile_cols)),
                col_landing(side).at[pl.ds(*middle)],
                *sends, 6 + place(side), device, side,
            )
        ]

    def col_end(side, row_side):
        return transfer(
            edges.at[place(row_side), place(side)],
            col_landing(side).at[pl.ds(*own_edge(row_side[0], tile_rows))],
            *sends, 8 + place(side) + 2 * place(row_side), device, side,
        )

    def col_ends(side):
        return [col_end(side, row_side) for row_side in ROW_SIDES]

    def edge_copy(row_side, side):
        start, count = own_edge(row_side[0], tile_rows)
        return pltpu.make_async_copy(
            at_region(halo, (start + REACH, count), outer_edge(side[1], tile_cols)),
            edges.at[place(row_side), place(side)],
            edge_sem.at[place(row_side) + 2 * place(side)],
        )

    for row_side in ROW_SIDES:
        for side in COL_SIDES:
            edge_copy(row_side, side).start()
    greet(inside, device)
    for side in ROW_SIDES:
        start_if(inside, side, lambda: corner_copies(side))
    for side in COL_SIDES:
        start_if(inside, side, lambda: col_middle(side))
    for side in ROW_SIDES:
        start_if(inside, side, lambda: row_copies(side))
    for row_side in ROW_SIDES:
        row = place(row_side)
        wait_recv_if(inside, opposite(row_side), lambda: corner_copies(opposite(row_side)))
        for side in COL_SIDES:
            col = place(side)
            edge_copy(row_side, side).wait()

            @pl.when(inside(row_side))
            def _():
                for i in range(REACH):
                    for j in range(REACH):
                        term = corners[row, col, i, j].astype(jnp.float32)
                        value = edges[row, col, i, j].astype(jnp.float32) + term
                        edges[row, col, i, j] = value.astype(edges.dtype)

            @pl.when(inside(side))
            def _():
                col_end(side, row_side).start()

    for side in ROW_SIDES:
        wait_recv_if(inside, side, lambda: row_copies(side))
        wait_send_if(inside, side, lambda: row_copies(side) + corner_copies(side))
    for side in COL_SIDES:
        wait_recv_if(inside, side, lambda: col_middle(side) + col_ends(side))
        wait_send_if(inside, side, lambda: col_middle(side) + col_ends(side))


def finish_kernel(own, *refs):
    landed, out, held, parts = refs[:4], refs[4], refs[5], refs[6:10]
    part_sem, load_sem, store_sem = refs[10:]
    landed_up, landed_down, landed_left, landed_right = parts
    tile_rows, tile_cols = own.shape[:2]
    inside, _ = neighbourhood()

    def load(i):
        return pltpu.make_async_copy(own.at[i], held.at[i], load_sem.at[i])

    def store(i):
        return pltpu.make_async_copy(held.at[i], out.at[i], store_sem.at[i])

    def fetch(index):
        return pltpu.make_async_copy(landed[index], parts[index], part_sem.at[index])

    load(0).start()
    for index in range(4):
        fetch(index).start()
    for i in range(1, tile_rows):
        load(i).start()
    for index in range(4):
        fetch(index).wait()
    for i in range(tile_rows):
        load(i).wait()
        for side, part in zip(COL_SIDES, (landed_left, landed_right)):
            start, count = own_edge(side[1], tile_cols)

            @pl.when(inside(side))
            def _():
                held[i, pl.ds(start, count)] += part[i].astype(jnp.float32)

        for side, part in zip(ROW_SIDES, (landed_up, landed_down)):
            start, count = own_edge(side[0], tile_rows)
            if start <= i < start + count:

                @pl.when(inside(side))
                def _():
                    held[i] += part[i - start].astype(jnp.float32)

        store(i).start()
    for i in range(tile_rows):
        store(i).wait()


def shards(rhs_blocks, diag_factor, cond_factor, cond):
    tile_rows, tile_cols, count_rhs, points = rhs_blocks.shape
    conds = cond.shape[2]
    depth = conds * points
    far = cond_factor.reshape(tile_rows, tile_cols, depth, points)
    codes = jnp.transpose(cond, (2, 0, 1))
    block = (count_rhs, points)
    padded = (tile_rows + 2 * REACH, tile_cols + 2 * REACH) + block
    outer = 2 * REACH
    inner = tile_cols - outer
    spread_shape = (tile_rows, inner, count_rhs, depth + points)
    anywhere = pl.BlockSpec(memory_space=pltpu.HBM)
    scalars = pl.BlockSpec(memory_space=pltpu.SMEM)
    whole = pl.BlockSpec(memory_space=pltpu.VMEM)
    transfers = 12
    white, spread = pl.pallas_call(
        forward_kernel,
        out_shape=(
            jax.ShapeDtypeStruct((tile_rows, outer) + block, jnp.bfloat16),
            jax.ShapeDtypeStruct(spread_shape, jnp.float32),
        ),
        in_specs=[anywhere, anywhere, anywhere, scalars],
        out_specs=(whole, anywhere),
        scratch_shapes=[
            pltpu.VMEM(rhs_blocks.shape, rhs_blocks.dtype),
            pltpu.VMEM((tile_rows + 2 * REACH, tile_cols) + block, rhs_blocks.dtype),
            pltpu.VMEM((tile_rows, tile_cols + 2 * REACH) + block, rhs_blocks.dtype),
            pltpu.VMEM(padded, rhs_blocks.dtype),
            pltpu.VMEM((tile_rows, tile_cols, depth + points, points), far.dtype),
            pltpu.VMEM(spread_shape, jnp.float32),
            pltpu.SemaphoreType.DMA((tile_rows,)),
            pltpu.SemaphoreType.DMA((tile_rows, 2)),
            pltpu.SemaphoreType.DMA((6,)),
            pltpu.SemaphoreType.DMA((transfers,)),
            pltpu.SemaphoreType.DMA((transfers,)),
        ],
        compiler_params=pltpu.CompilerParams(
            collective_id=0, has_side_effects=True, vmem_limit_bytes=63 * 2**20
        ),
        name="forward",
    )(rhs_blocks, diag_factor, far, codes)

    own, halo = pl.pallas_call(
        backward_kernel,
        out_shape=(
            jax.ShapeDtypeStruct(rhs_blocks.shape, jnp.float32),
            jax.ShapeDtypeStruct(padded, jnp.bfloat16),
        ),
        in_specs=[whole, anywhere, anywhere, anywhere, scalars],
        out_specs=(anywhere, anywhere),
        scratch_shapes=[
            pltpu.VMEM((tile_rows, outer, depth + points, points), far.dtype),
            pltpu.VMEM(spread_shape, jnp.float32),
            pltpu.VMEM(padded, jnp.float32),
            pltpu.VMEM(rhs_blocks.shape, jnp.float32),
            pltpu.VMEM(padded, jnp.bfloat16),
            pltpu.SemaphoreType.DMA((tile_rows, 5)),
            pltpu.SemaphoreType.DMA((tile_rows,)),
            pltpu.SemaphoreType.DMA((tile_rows + 2 * REACH,)),
        ],
        compiler_params=pltpu.CompilerParams(vmem_limit_bytes=63 * 2**20),
        name="backward",
    )(white, diag_factor, far, spread, codes)

    row_part = jax.ShapeDtypeStruct((REACH, tile_cols) + block, jnp.bfloat16)
    col_part = jax.ShapeDtypeStruct((tile_rows, REACH) + block, jnp.bfloat16)
    landed = pl.pallas_call(
        exchange_kernel,
        out_shape=(row_part, row_part, col_part, col_part),
        in_specs=[anywhere],
        out_specs=(anywhere,) * 4,
        scratch_shapes=[
            pltpu.VMEM((2, 2, REACH, REACH) + block, jnp.bfloat16),
            pltpu.VMEM((2, 2, REACH, REACH) + block, jnp.bfloat16),
            pltpu.SemaphoreType.DMA((4,)),
            pltpu.SemaphoreType.DMA((transfers,)),
            pltpu.SemaphoreType.DMA((transfers,)),
        ],
        compiler_params=pltpu.CompilerParams(
            collective_id=1, has_side_effects=True, vmem_limit_bytes=63 * 2**20
        ),
        name="exchange",
    )(halo)

    return pl.pallas_call(
        finish_kernel,
        out_shape=jax.ShapeDtypeStruct(rhs_blocks.shape, jnp.float32),
        in_specs=[anywhere] * 5,
        out_specs=anywhere,
        scratch_shapes=[
            pltpu.VMEM(rhs_blocks.shape, jnp.float32),
            pltpu.VMEM(row_part.shape, row_part.dtype),
            pltpu.VMEM(row_part.shape, row_part.dtype),
            pltpu.VMEM(col_part.shape, col_part.dtype),
            pltpu.VMEM(col_part.shape, col_part.dtype),
            pltpu.SemaphoreType.DMA((4,)),
            pltpu.SemaphoreType.DMA((tile_rows,)),
            pltpu.SemaphoreType.DMA((tile_rows,)),
        ],
        compiler_params=pltpu.CompilerParams(vmem_limit_bytes=63 * 2**20),
        name="finish",
    )(own, *landed)


def solution(mesh):
    in_specs = (
        P("gx", "gy", None, None),
        P("gx", "gy", None, None),
        P("gx", "gy", None, None, None),
        P("gx", "gy", None),
    )
    out_specs = P("gx", "gy", None, None)
    return jax.shard_map(shards, mesh=mesh, in_specs=in_specs, out_specs=out_specs, check_vma=False)
```
